128 devices in a mesh: freq: 4 (over x), pts: 32 (over z, y, core).
Axes of the slice: x: 4, y: 4, z: 4, core: 2. Of those that a mesh axis runs over, the one named last changes fastest.
Arguments:
- snapshots: bfloat16 [131072, 4224], P(('freq', 'pts')), as said below
- weights: float32 [131072], P(('freq', 'pts')), may hold values from 0.25 to 4
- freq_bins: int32 [8], replicated, may hold values from 1 to 127
Outputs:
- spod_modes: float32 [2, 8, 32, 131072], P(None, None, None, ('freq', 'pts'))
- upper_factor: float32 [2, 8, 32, 32], P(None, 'freq')
The draws below stay inside these ranges and needn't reach their ends.
Inputs may be any that keep to these rules, and one draw needn't show every extreme that they name: `snapshots`: fluctuations of pressure and velocity, with a few motions coherent over many points.
All inputs are finite; a program needn't handle non-finite values.
Results may differ from the reference program's by a relative error of at most 0.0045.
Values sent between devices are 32-bit elements; how exact they have to be, the bound alone decides.
A program may use at most 64 MiB of HBM per device.

```python
import math
import jax
import jax.numpy as jnp
from jax import lax

FREQ = 8
NB = 32
NFFT = 256
SAMPLES = 4224
POINTS = 131072


def draw_snapshots(key, part):
    keys = jax.random.split(key, 3)
    noise_field = jax.random.normal(keys[0], (POINTS, SAMPLES), jnp.float32)
    coupling = jax.random.normal(keys[1], (POINTS, 4), jnp.float32)
    signals = jax.random.normal(keys[2], (4, SAMPLES), jnp.float32)
    result = noise_field
    for motion in range(4):
        result = result + coupling[:, motion:motion + 1] * signals[motion][None, :]
    return result.astype(jnp.bfloat16)


def plant(drawn, rng, least, high):
    longest = drawn.shape.index(max(drawn.shape))
    spots = []
    for shift in (0, 1):
        where = [jax.random.randint(jax.random.fold_in(rng, axis), (), 0, length) for axis, length in enumerate(drawn.shape)]
        where[longest] = (where[longest] + shift) % drawn.shape[longest]
        spots.append(tuple(where))
    return drawn.at[spots[0]].set(least).at[spots[1]].set(high)


def block_scale(stream_key, shape, cuts, least, largest):
    def one(axis_at, blocks):
        heights = jax.random.uniform(jax.random.fold_in(jax.random.fold_in(stream_key, 6), axis_at), (blocks,), jnp.float32, least / len(cuts), largest / len(cuts))
        return jnp.repeat(jnp.exp(heights), shape[axis_at] // blocks).reshape((-1,) + (1,) * (len(shape) - axis_at - 1))

    loudness = one(*cuts[0])
    for cut in cuts[1:]:
        loudness = loudness * one(*cut)
    return loudness


def setup_inputs(seed: int = 0) -> dict:
    key_of = jax.random.split(jax.random.key(seed), 4)
    snapshots = draw_snapshots(jax.random.fold_in(key_of[3], 71), 0)
    weights = jnp.clip(jnp.exp(math.log(4.0) - 2.7725887 * jax.random.uniform(key_of[1], (POINTS,), jnp.float32) ** block_scale(key_of[1], (POINTS,), ((0, 128),), -0.2, 0.2)), 0.25, 4.0)
    freq_bins = plant(jax.random.randint(key_of[2], (FREQ,), 1, NFFT // 2), jax.random.fold_in(key_of[2], 1), 1, (NFFT // 2) - 1).astype(jnp.int32)
    return dict(snapshots=snapshots, weights=weights, freq_bins=freq_bins)


def dft_tables(freq_bins):
    moments = jnp.arange(NFFT, dtype=jnp.int32)
    phase_index = freq_bins[:, None] * moments[None, :] % NFFT
    angle = phase_index.astype(jnp.float32) * (2.0 * math.pi / NFFT)
    window = 0.5 - 0.5 * jnp.cos(moments.astype(jnp.float32) * (2.0 * math.pi / NFFT))
    table = jnp.concatenate([window[None, :] * jnp.cos(angle), -window[None, :] * jnp.sin(angle)], axis=0)
    return table.astype(jnp.bfloat16)

def transform(snap_block, freq_bins):
    point_count = snap_block.shape[0]
    half_len = NFFT // 2
    dft_table = dft_tables(freq_bins)
    halves = snap_block.reshape(point_count, NB + 1, half_len).astype(jnp.float32)
    table_wide = dft_table.astype(jnp.float32)
    front_part = jnp.einsum('ct,pbt->cbp', table_wide[:, :half_len], halves, precision=lax.Precision.HIGHEST)
    second = jnp.einsum('ct,pbt->cbp', table_wide[:, half_len:], halves, precision=lax.Precision.HIGHEST)
    coefficients = front_part[:, :NB] + second[:, 1:]
    point_mean = lax.optimization_barrier(jnp.sum(snap_block, axis=1, dtype=jnp.float32)) / snap_block.shape[1]
    table_sum = lax.optimization_barrier(jnp.sum(table_wide, axis=1))
    coefficients = (coefficients - table_sum[:, None, None] * point_mean[None, None, :]) * (1.0 / math.sqrt(NB * 0.375 * NFFT))
    return coefficients.reshape(2, FREQ, NB, point_count)

def gram_matrix(part_real, part_imag):
    gram_real = jnp.einsum('fbp,fcp->fbc', part_real, part_real, precision=lax.Precision.HIGHEST)
    gram_real = gram_real + jnp.einsum('fbp,fcp->fbc', part_imag, part_imag, precision=lax.Precision.HIGHEST)
    cross = jnp.einsum('fbp,fcp->fbc', part_real, part_imag, precision=lax.Precision.HIGHEST)
    return (gram_real, cross - jnp.swapaxes(cross, 1, 2))

def cholesky_upper(gram_real, gram_imag):
    order = gram_real.shape[-1]
    columns = jnp.arange(order)

    def one_row(row_index, state_pair):
        upper_real, upper_imag = state_pair
        col_real = lax.dynamic_slice_in_dim(upper_real, row_index, 1, 2)
        col_imag = lax.dynamic_slice_in_dim(upper_imag, row_index, 1, 2)
        sum_real = lax.optimization_barrier(jnp.sum(col_real * upper_real + col_imag * upper_imag, axis=1))
        sum_imag = lax.optimization_barrier(jnp.sum(col_real * upper_imag - col_imag * upper_real, axis=1))
        rest_real = lax.dynamic_slice_in_dim(gram_real, row_index, 1, 1)[:, 0, :] - sum_real
        rest_imag = lax.dynamic_slice_in_dim(gram_imag, row_index, 1, 1)[:, 0, :] - sum_imag
        pivot = jnp.sqrt(lax.dynamic_slice_in_dim(rest_real, row_index, 1, 1))
        above_diag = columns[None, :] > row_index
        on_diag = columns[None, :] == row_index
        new_real = jnp.where(above_diag, rest_real / pivot, 0.0) + jnp.where(on_diag, pivot, 0.0)
        new_imag = jnp.where(above_diag, rest_imag / pivot, 0.0)
        upper_real = lax.dynamic_update_slice_in_dim(upper_real, new_real[:, None, :], row_index, 1)
        upper_imag = lax.dynamic_update_slice_in_dim(upper_imag, new_imag[:, None, :], row_index, 1)
        return (upper_real, upper_imag)
    zeros = jnp.zeros_like(gram_real)
    return lax.fori_loop(0, order, one_row, (zeros, zeros))

def inverse_upper(upper_real, upper_imag):
    order = upper_real.shape[-1]
    columns = jnp.arange(order)
    identity = jnp.eye(order, dtype=upper_real.dtype)

    def one_row(step_index, state_pair):
        inv_real, inv_imag = state_pair
        row_index = order - 1 - step_index
        row_real = lax.dynamic_slice_in_dim(upper_real, row_index, 1, 1)[:, 0, :]
        row_imag = lax.dynamic_slice_in_dim(upper_imag, row_index, 1, 1)[:, 0, :]
        above_diag = columns[None, :] > row_index
        off_real = jnp.where(above_diag, row_real, 0.0)
        off_imag = jnp.where(above_diag, row_imag, 0.0)
        sum_real = lax.optimization_barrier(jnp.sum(off_real[:, :, None] * inv_real - off_imag[:, :, None] * inv_imag, axis=1))
        sum_imag = lax.optimization_barrier(jnp.sum(off_real[:, :, None] * inv_imag + off_imag[:, :, None] * inv_real, axis=1))
        pivot = lax.dynamic_slice_in_dim(row_real, row_index, 1, 1)
        unit_row = lax.dynamic_slice_in_dim(identity, row_index, 1, 0)
        new_real = (unit_row - sum_real) / pivot
        new_imag = -sum_imag / pivot
        inv_real = lax.dynamic_update_slice_in_dim(inv_real, new_real[:, None, :], row_index, 1)
        inv_imag = lax.dynamic_update_slice_in_dim(inv_imag, new_imag[:, None, :], row_index, 1)
        return (inv_real, inv_imag)
    zeros = jnp.zeros_like(upper_real)
    return lax.fori_loop(0, order, one_row, (zeros, zeros))

def recover(inv_real, inv_imag, part_real, part_imag, all_points):
    mode_real = jnp.einsum('fbc,fbp->fcp', inv_real, part_real, precision=lax.Precision.HIGHEST)
    mode_real = mode_real - jnp.einsum('fbc,fbp->fcp', inv_imag, part_imag, precision=lax.Precision.HIGHEST)
    mode_imag = jnp.einsum('fbc,fbp->fcp', inv_imag, part_real, precision=lax.Precision.HIGHEST)
    mode_imag = mode_imag + jnp.einsum('fbc,fbp->fcp', inv_real, part_imag, precision=lax.Precision.HIGHEST)
    return jnp.stack([mode_real, mode_imag]) * math.sqrt(all_points)

def reference(snapshots, weights, freq_bins):
    block_len = math.gcd(POINTS, 4096)
    grouped = snapshots.reshape(POINTS // block_len, block_len, SAMPLES)
    pieces = lax.map(lambda piece: transform(piece, freq_bins), grouped)
    coefficients = jnp.moveaxis(pieces, 0, 3).reshape(2, FREQ, NB, POINTS)
    scaled = coefficients * jnp.sqrt(weights / POINTS)[None, None, None, :]
    gram_real, gram_imag = gram_matrix(scaled[0], scaled[1])
    upper_real, upper_imag = cholesky_upper(gram_real, gram_imag)
    inv_real, inv_imag = inverse_upper(upper_real, upper_imag)
    spod_modes = recover(inv_real, inv_imag, scaled[0], scaled[1], POINTS)
    return (spod_modes, jnp.stack([upper_real, upper_imag]))
```

```python
import math

import jax
import jax.numpy as jnp
from jax import lax
from jax.experimental import pallas as pl
from jax.experimental.pallas import tpu as pltpu
from jax.sharding import PartitionSpec as P

FREQ = 8
NB = 32
NFFT = 256
HALF = NFFT // 2
SAMPLES = 4224
POINTS = 131072
LOCAL = 1024
CHUNK = 256
CHUNKS = LOCAL // CHUNK
GROUPS = 4
BAND = 9 * HALF
ROWS = 144
OWNERS = 8
SHARES = 16
MESH = pl.DeviceIdType.MESH
F32 = jnp.float32
BF16 = jnp.bfloat16
NT = (((1,), (1,)), ((), ()))


def place():
    x = lax.axis_index("freq")
    q = lax.axis_index("pts")
    core = lax.rem(q, 2)
    share = lax.div(q, 2)
    owner = x * 2 + core
    return owner, share


def device_of(owner, share):
    return (lax.div(owner, 2), share * 2 + lax.rem(owner, 2))


def owner_peer(owner, share, step):
    other = lax.rem(owner + step, OWNERS)
    return other, device_of(other, share)


def share_peer(owner, share, step):
    other = lax.rem(share + step, SHARES)
    return other, device_of(owner, other)


def build_band(bins_ref, band_ref, sums_ref):
    row = lax.broadcasted_iota(jnp.int32, (FREQ, NFFT), 0)
    moment = lax.broadcasted_iota(jnp.int32, (FREQ, NFFT), 1)
    bins = jnp.zeros((FREQ, NFFT), jnp.int32)
    for f in range(FREQ):
        bins = jnp.where(row == f, bins_ref[f], bins)
    angle = lax.bitwise_and(bins * moment, NFFT - 1).astype(F32) * (2.0 * math.pi / NFFT)
    window = 0.5 - 0.5 * jnp.cos(moment.astype(F32) * (2.0 * math.pi / NFFT))
    cosine = (window * jnp.cos(angle)).astype(BF16).astype(F32)
    sine = (-window * jnp.sin(angle)).astype(BF16).astype(F32)
    slot = lax.broadcasted_iota(jnp.int32, (8, HALF), 0)
    for q in range(9):
        tiles = []
        for c in range(2 * FREQ):
            table = cosine if c < FREQ else sine
            line = table[c % FREQ : c % FREQ + 1]
            front = jnp.broadcast_to(line[:, :HALF], (8, HALF))
            back = jnp.broadcast_to(line[:, HALF:], (8, HALF))
            tiles.append(jnp.where(slot == q, front, jnp.where(slot == q - 1, back, 0.0)))
        mark = 0 if q < 8 else 1
        tiles.append(jnp.where(slot == mark, 1.0, 0.0))
        tiles.append(jnp.zeros((8, HALF), F32))
        band_ref[:, q * HALF : (q + 1) * HALF] = jnp.concatenate(tiles, axis=0).astype(BF16)
    ones = jnp.ones((BAND, 128), BF16)
    sums_ref[...] = jnp.dot(band_ref[0:128, :], ones, preferred_element_type=F32)


def transform_chunk(chunk, weights_ref, x_ref, band_ref, sums_ref, parts_ref):
    band = band_ref[...]
    groups = []
    total = jnp.zeros((1, CHUNK), F32)
    for g in range(GROUPS):
        x = x_ref[chunk, :, g * 8 * HALF : g * 8 * HALF + BAND]
        d = lax.dot_general(band, x, NT, preferred_element_type=F32)
        groups.append(d)
        total = total + d[128:129]
        if g == GROUPS - 1:
            total = total + d[129:130]
    mean = total * (1.0 / SAMPLES)
    w = jnp.concatenate([weights_ref[2 * chunk : 2 * chunk + 1], weights_ref[2 * chunk + 1 : 2 * chunk + 2]], axis=1)
    scale = jnp.sqrt(w * (1.0 / POINTS)) * (1.0 / math.sqrt(NB * 0.375 * NFFT))
    cols = slice(chunk * CHUNK, (chunk + 1) * CHUNK)
    for f in range(FREQ):
        for part in range(2):
            c = part * FREQ + f
            sums = sums_ref[c * 8 : c * 8 + 8, :]
            away = jnp.concatenate([sums, sums], axis=1) * mean
            y = jnp.concatenate([(d[c * 8 : c * 8 + 8] - away) * scale for d in groups], axis=0)
            hi = y.astype(BF16)
            lo = (y - hi.astype(F32)).astype(BF16)
            parts_ref[f, part * NB : (part + 1) * NB, cols] = hi
            parts_ref[f, 64 + part * NB : 64 + (part + 1) * NB, cols] = lo
            parts_ref[f, 128 + part * NB : 128 + (part + 1) * NB, cols] = hi


def packed_gram(parts_ref, f):
    hi = parts_ref[f, 0:64, :]
    lo = parts_ref[f, 64:128, :]
    s = lax.dot_general(hi, hi, NT, preferred_element_type=F32)
    s = s + lax.dot_general(hi, lo, NT, preferred_element_type=F32)
    s = s + lax.dot_general(lo, hi, NT, preferred_element_type=F32)
    gram_real = s[0:32, 0:32] + s[32:64, 32:64]
    gram_imag = s[0:32, 32:64] - s[32:64, 0:32]
    i = lax.broadcasted_iota(jnp.int32, (NB, NB), 0)
    j = lax.broadcasted_iota(jnp.int32, (NB, NB), 1)
    packed = jnp.where(i >= j, gram_real, gram_imag)
    return jnp.concatenate([packed[8 * r : 8 * r + 8] for r in range(4)], axis=1)


def eliminate(packed):
    p = jnp.concatenate([packed[:, 32 * r : 32 * r + 32] for r in range(4)], axis=0)
    t = p.T
    i = lax.broadcasted_iota(jnp.int32, (NB, NB), 0)
    j = lax.broadcasted_iota(jnp.int32, (NB, NB), 1)
    real = jnp.where(i >= j, p, t)
    imag = jnp.where(i < j, p, jnp.where(i > j, -t, 0.0))
    eye = jnp.where(i == j, 1.0, 0.0)
    zero = jnp.zeros((NB, NB), F32)
    whole = jnp.concatenate([real, imag, eye, zero], axis=1)
    turned = jnp.concatenate([-imag, real, zero, eye], axis=1)
    a = [whole[8 * u : 8 * u + 8] for u in range(4)]
    b = [turned[8 * u : 8 * u + 8] for u in range(4)]
    pivots = [jnp.ones((8, 128), F32) for u in range(4)]
    sub = lax.broadcasted_iota(jnp.int32, (8, 128), 0)
    for k in range(NB):
        v, s = k // 8, k % 8
        col_real = {u: jnp.broadcast_to(a[u][:, k : k + 1], (8, 128)) for u in range(v, 4)}
        col_imag = {u: jnp.broadcast_to(a[u][:, 32 + k : 33 + k], (8, 128)) for u in range(v, 4)}
        pivot = jnp.broadcast_to(col_real[v][s : s + 1], (8, 128))
        over = 1.0 / pivot
        row = jnp.broadcast_to(a[v][s : s + 1], (8, 128)) * over
        row_turned = jnp.broadcast_to(b[v][s : s + 1], (8, 128)) * over
        pivots[v] = jnp.where(sub == s, pivot, pivots[v])
        for u in range(v, 4):
            m_real, m_imag = col_real[u], col_imag[u]
            if u == v:
                m_real = jnp.where(sub > s, m_real, 0.0)
                m_imag = jnp.where(sub > s, m_imag, 0.0)
            a[u], b[u] = (
                a[u] - (m_real * row + m_imag * row_turned),
                b[u] - (m_real * row_turned - m_imag * row),
            )
    return [a[u] * (1.0 / jnp.sqrt(pivots[u])) for u in range(4)]


def wait_bytes(ref, sem):
    pltpu.make_async_copy(ref, ref, sem).wait()


def kernel(
    bins_ref, weights_ref, snap_ref, modes_ref, upper_ref,
    x_ref, band_ref, sums_ref, parts_ref, out_ref, pack_ref, got_a, got_b, got_c, got_r,
    in_sem, out_sem, send_a, recv_a, send_b, recv_b, send_c, recv_c, send_r, recv_r,
):
    owner, share = place()
    core = lax.rem(owner, 2)
    loads = []
    for chunk in range(CHUNKS):
        load = pltpu.make_async_copy(snap_ref.at[chunk * CHUNK : (chunk + 1) * CHUNK, :], x_ref.at[chunk], in_sem.at[chunk])
        load.start()
        loads.append(load)
    barrier = pltpu.get_barrier_semaphore()
    for step in range(1, OWNERS):
        pl.semaphore_signal(barrier, inc=1, device_id=owner_peer(owner, share, step)[1], device_id_type=MESH)
    for step in range(1, SHARES):
        pl.semaphore_signal(barrier, inc=1, device_id=share_peer(owner, share, step)[1], device_id_type=MESH)

    build_band(bins_ref, band_ref, sums_ref)
    for chunk in range(CHUNKS):
        loads[chunk].wait()
        transform_chunk(chunk, weights_ref, x_ref, band_ref, sums_ref, parts_ref)
    for f in range(FREQ):
        pack_ref[f] = packed_gram(parts_ref, f)

    pl.semaphore_wait(barrier, OWNERS - 1 + SHARES - 1)
    for step in range(1, OWNERS):
        other, device = owner_peer(owner, share, step)
        pltpu.make_async_remote_copy(
            src_ref=pack_ref.at[other], dst_ref=got_a.at[owner], send_sem=send_a, recv_sem=recv_a,
            device_id=device, device_id_type=MESH,
        ).start()
    got_a[owner] = pack_ref[owner]
    wait_bytes(got_a.at[0 : OWNERS - 1], recv_a)
    part = got_a[0]
    for n in range(1, OWNERS):
        part = part + got_a[n]

    got_b[share] = part
    for step in range(1, SHARES):
        other, device = share_peer(owner, share, step)
        pltpu.make_async_remote_copy(
            src_ref=got_b.at[share], dst_ref=got_b.at[share], send_sem=send_b, recv_sem=recv_b,
            device_id=device, device_id_type=MESH,
        ).start()
    wait_bytes(got_b.at[0 : SHARES - 1], recv_b)
    packed = got_b[0]
    for n in range(1, SHARES):
        packed = packed + got_b[n]

    rows = eliminate(packed)
    lane = lax.broadcasted_iota(jnp.int32, (8, 128), 1)
    for h in range(2):
        even, odd = rows[2 * h], rows[2 * h + 1]
        odd_far = pltpu.roll(odd, 64, 1)
        got_c[owner, h] = jnp.where(lane < 64, odd_far, even)
        got_r[core, h] = jnp.where(lane < 64, even, odd_far)
    for step in range(1, OWNERS):
        other, device = owner_peer(owner, share, step)
        pltpu.make_async_remote_copy(
            src_ref=got_c.at[owner], dst_ref=got_c.at[owner], send_sem=send_c, recv_sem=recv_c,
            device_id=device, device_id_type=MESH,
        ).start()
    x = lax.div(owner, 2)
    pltpu.make_async_remote_copy(
        src_ref=got_r.at[core], dst_ref=got_r.at[core], send_sem=send_r, recv_sem=recv_r,
        device_id=(x, share * 2 + 1 - core), device_id_type=MESH,
    ).start()
    wait_bytes(got_c.at[0 : OWNERS - 1], recv_c)

    stores = []
    for f in range(FREQ):
        inv = jnp.concatenate(
            [got_c[f, 0][:, 64:], got_c[f, 0][:, :64], got_c[f, 1][:, 64:], got_c[f, 1][:, :64]], axis=0
        ) * math.sqrt(POINTS)
        inv = jnp.concatenate([inv, jnp.concatenate([-inv[:, 32:], inv[:, :32]], axis=1)], axis=0)
        hi = inv.astype(BF16)
        lo = (inv - hi.astype(F32)).astype(BF16)
        left = jnp.concatenate([hi, hi, lo], axis=1)
        modes = jnp.dot(left, parts_ref[f], preferred_element_type=F32)
        out_ref[0, f] = modes[0:32]
        out_ref[1, f] = modes[32:64]
        store = pltpu.make_async_copy(out_ref.at[:, f], modes_ref.at[:, f], out_sem.at[f])
        store.start()
        stores.append(store)

    wait_bytes(got_r.at[0], recv_r)
    i = lax.broadcasted_iota(jnp.int32, (NB, NB), 0)
    j = lax.broadcasted_iota(jnp.int32, (NB, NB), 1)
    for n in range(2):
        both = jnp.concatenate(
            [got_r[n, 0][:, :64], got_r[n, 0][:, 64:], got_r[n, 1][:, :64], got_r[n, 1][:, 64:]], axis=0
        )
        upper_ref[0, n] = jnp.where(j >= i, both[:, :32], 0.0)
        upper_ref[1, n] = jnp.where(j > i, both[:, 32:], 0.0)
    wait_bytes(got_a.at[0 : OWNERS - 1], send_a)
    wait_bytes(got_b.at[0 : SHARES - 1], send_b)
    wait_bytes(got_c.at[0 : OWNERS - 1], send_c)
    wait_bytes(got_r.at[0], send_r)
    for store in stores:
        store.wait()


def body(snapshots, weights, freq_bins):
    dma = pltpu.SemaphoreType.DMA
    return pl.pallas_call(
        kernel,
        out_shape=(
            jax.ShapeDtypeStruct((2, FREQ, NB, LOCAL), F32),
            jax.ShapeDtypeStruct((2, 2, NB, NB), F32),
        ),
        in_specs=[
            pl.BlockSpec(memory_space=pltpu.SMEM),
            pl.BlockSpec(memory_space=pltpu.VMEM),
            pl.BlockSpec(memory_space=pltpu.HBM),
        ],
        out_specs=(pl.BlockSpec(memory_space=pltpu.HBM), pl.BlockSpec(memory_space=pltpu.VMEM)),
        scratch_shapes=[
            pltpu.VMEM((CHUNKS, CHUNK, SAMPLES), BF16),
            pltpu.VMEM((ROWS, BAND), BF16),
            pltpu.VMEM((128, 128), F32),
            pltpu.VMEM((FREQ, 192, LOCAL), BF16),
            pltpu.VMEM((2, FREQ, NB, LOCAL), F32),
            pltpu.VMEM((FREQ, 8, 128), F32),
            pltpu.VMEM((OWNERS, 8, 128), F32),
            pltpu.VMEM((SHARES, 8, 128), F32),
            pltpu.VMEM((OWNERS, 2, 8, 128), F32),
            pltpu.VMEM((2, 2, 8, 128), F32),
            dma((CHUNKS,)), dma((FREQ,)),
            dma, dma, dma, dma, dma, dma, dma, dma,
        ],
        compiler_params=pltpu.CompilerParams(
            collective_id=0, has_side_effects=True, vmem_limit_bytes=60 * 1024 * 1024
        ),
        cost_estimate=pl.CostEstimate(flops=2_000_000_000, bytes_accessed=11_000_000, transcendentals=0),
    )(freq_bins, weights.reshape(8, 128), snapshots)


def solution(mesh):
    return jax.shard_map(
        body,
        mesh=mesh,
        in_specs=(P(("freq", "pts"), None), P(("freq", "pts")), P()),
        out_specs=(P(None, None, None, ("freq", "pts")), P(None, "freq", None, None)),
        check_vma=False,
    )
```

```python
import math

import jax
import jax.numpy as jnp
from jax import lax
from jax.experimental import pallas as pl
from jax.experimental.pallas import tpu as pltpu
from jax.sharding import PartitionSpec as P

FREQ = 8
NB = 32
NFFT = 256
HALF = NFFT // 2
SAMPLES = 4224
POINTS = 131072
LOCAL = 1024
CHUNK = 256
CHUNKS = LOCAL // CHUNK
GROUPS = 4
BAND = 9 * HALF
ROWS = 144
ROW = 4
SHARES = 16
WIDTH = 4
GRAM_MIB = 44
MODES_MIB = 40
ROW_STEPS = (2, 1, 3)
PLANE_STEPS = (10, 6, 9, 11, 14, 2, 5, 7, 8, 13, 15, 1, 3, 4, 12)
MESH = pl.DeviceIdType.MESH
F32 = jnp.float32
BF16 = jnp.bfloat16
NT = (((1,), (1,)), ((), ()))


def place():
    x = lax.axis_index("freq")
    q = lax.axis_index("pts")
    return x, lax.div(q, 2), lax.rem(q, 2)


def row_peer(x, share, core, step):
    other = lax.rem(x + step, ROW)
    return other, (other, share * 2 + core)


def plane_peer(x, share, core, step):
    z, y = lax.div(share, 4), lax.rem(share, 4)
    other = lax.rem(z + step // 4, 4) * 4 + lax.rem(y + step % 4, 4)
    return other, (x, other * 2 + core)


def build_band(bins_ref, band_ref, sums_ref):
    row = lax.broadcasted_iota(jnp.int32, (FREQ, NFFT), 0)
    moment = lax.broadcasted_iota(jnp.int32, (FREQ, NFFT), 1)
    bins = jnp.zeros((FREQ, NFFT), jnp.int32)
    for f in range(FREQ):
        bins = jnp.where(row == f, bins_ref[f], bins)
    angle = lax.bitwise_and(bins * moment, NFFT - 1).astype(F32) * (2.0 * math.pi / NFFT)
    window = 0.5 - 0.5 * jnp.cos(moment.astype(F32) * (2.0 * math.pi / NFFT))
    cosine = (window * jnp.cos(angle)).astype(BF16).astype(F32)
    sine = (-window * jnp.sin(angle)).astype(BF16).astype(F32)
    slot = lax.broadcasted_iota(jnp.int32, (8, HALF), 0)
    for q in range(9):
        tiles = []
        for c in range(2 * FREQ):
            table = cosine if c < FREQ else sine
            line = table[c % FREQ : c % FREQ + 1]
            front = jnp.broadcast_to(line[:, :HALF], (8, HALF))
            back = jnp.broadcast_to(line[:, HALF:], (8, HALF))
            tiles.append(jnp.where(slot == q, front, jnp.where(slot == q - 1, back, 0.0)))
        mark = 0 if q < 8 else 1
        tiles.append(jnp.where(slot == mark, 1.0, 0.0))
        tiles.append(jnp.zeros((8, HALF), F32))
        band_ref[:, q * HALF : (q + 1) * HALF] = jnp.concatenate(tiles, axis=0).astype(BF16)
    ones = jnp.ones((BAND, 128), BF16)
    sums_ref[...] = jnp.dot(band_ref[0:128, :], ones, preferred_element_type=F32)


def transform_chunk(chunk, weights_ref, x_ref, band_ref, sums_ref, parts_ref):
    band = band_ref[...]
    groups = []
    total = jnp.zeros((1, CHUNK), F32)
    for g in range(GROUPS):
        x = x_ref[chunk, :, g * 8 * HALF : g * 8 * HALF + BAND]
        d = lax.dot_general(band, x, NT, preferred_element_type=F32)
        groups.append(d)
        total = total + d[128:129]
        if g == GROUPS - 1:
            total = total + d[129:130]
    mean = total * (1.0 / SAMPLES)
    w = jnp.concatenate([weights_ref[2 * chunk : 2 * chunk + 1], weights_ref[2 * chunk + 1 : 2 * chunk + 2]], axis=1)
    scale = jnp.sqrt(w * (1.0 / POINTS)) * (1.0 / math.sqrt(NB * 0.375 * NFFT))
    cols = slice(chunk * CHUNK, (chunk + 1) * CHUNK)
    for f in range(FREQ):
        for part in range(2):
            c = part * FREQ + f
            sums = sums_ref[c * 8 : c * 8 + 8, :]
            away = jnp.concatenate([sums, sums], axis=1) * mean
            y = jnp.concatenate([(d[c * 8 : c * 8 + 8] - away) * scale for d in groups], axis=0)
            hi = y.astype(BF16)
            lo = (y - hi.astype(F32)).astype(BF16)
            parts_ref[f, part * NB : (part + 1) * NB, cols] = hi
            parts_ref[f, 64 + part * NB : 64 + (part + 1) * NB, cols] = lo
            parts_ref[f, 128 + part * NB : 128 + (part + 1) * NB, cols] = hi


def add_gram(parts_ref, gram_ref, chunk):
    cols = slice(chunk * CHUNK, (chunk + 1) * CHUNK)
    for f in range(FREQ):
        hi = parts_ref[f, 0:64, cols]
        lo = parts_ref[f, 64:128, cols]
        s = lax.dot_general(hi, hi, NT, preferred_element_type=F32)
        s = s + lax.dot_general(hi, lo, NT, preferred_element_type=F32)
        s = s + lax.dot_general(lo, hi, NT, preferred_element_type=F32)
        gram_ref[f] = s if chunk == 0 else gram_ref[f] + s


def packed_gram(gram_ref, f):
    s = gram_ref[f]
    gram_real = s[0:32, 0:32] + s[32:64, 32:64]
    gram_imag = s[0:32, 32:64] - s[32:64, 0:32]
    i = lax.broadcasted_iota(jnp.int32, (NB, NB), 0)
    j = lax.broadcasted_iota(jnp.int32, (NB, NB), 1)
    packed = jnp.where(i >= j, gram_real, gram_imag)
    return jnp.concatenate([packed[8 * r : 8 * r + 8] for r in range(4)], axis=1)


def lanes(tile, k):
    return jnp.broadcast_to(tile[:, k : k + 1], (8, 128))


def sublanes(tile, s):
    return jnp.broadcast_to(tile[s : s + 1], (8, 128))


def unpack_gram(packed):
    p = jnp.concatenate([packed[:, 32 * r : 32 * r + 32] for r in range(4)], axis=0)
    t = p.T
    i = lax.broadcasted_iota(jnp.int32, (NB, NB), 0)
    j = lax.broadcasted_iota(jnp.int32, (NB, NB), 1)
    real = jnp.where(i >= j, p, t)
    imag = jnp.where(i < j, p, jnp.where(i > j, -t, 0.0))
    eye = jnp.where(i == j, 1.0, 0.0)
    zero = jnp.zeros((NB, NB), F32)
    whole = jnp.concatenate([real, imag, eye, zero], axis=1)
    turned = jnp.concatenate([-imag, real, zero, eye], axis=1)
    return [whole[8 * u : 8 * u + 8] for u in range(4)], [turned[8 * u : 8 * u + 8] for u in range(4)]


def eliminate(packed):
    a, b = unpack_gram(packed)
    pivots = [jnp.ones((8, 128), F32) for _ in range(4)]
    sub = lax.broadcasted_iota(jnp.int32, (8, 128), 0)
    for first in range(0, NB, WIDTH):
        v, s = first // 8, first % 8
        last = s + WIDTH == 8
        col_real = {u: [lanes(a[u], first + j) for j in range(WIDTH)] for u in range(v, 4)}
        col_imag = {u: [lanes(a[u], NB + first + j) for j in range(WIDTH)] for u in range(v, 4)}
        rows = [sublanes(a[v], s + j) for j in range(WIDTH)]
        turned = [sublanes(b[v], s + j) for j in range(WIDTH)]
        block_real = [[sublanes(col_real[v][l], s + i) for l in range(i + 1)] for i in range(WIDTH)]
        block_imag = [[sublanes(col_imag[v][l], s + i) for l in range(i)] for i in range(WIDTH)]
        over = []
        for j in range(WIDTH):
            pivot = block_real[j][j]
            inverse = 1.0 / pivot
            over.append(inverse)
            pivots[v] = jnp.where(sub == s + j, pivot, pivots[v])
            below = range(j + 1, WIDTH)
            m_real = {i: block_real[i][j] * inverse for i in below}
            m_imag = {i: block_imag[i][j] * inverse for i in below}
            for i in below:
                for l in range(j + 1, i + 1):
                    other_real, other_imag = block_real[l][j], block_imag[l][j]
                    block_real[i][l] = block_real[i][l] - (m_real[i] * other_real + m_imag[i] * other_imag)
                    if l < i:
                        block_imag[i][l] = block_imag[i][l] - (m_imag[i] * other_real - m_real[i] * other_imag)
            for i in below:
                rows[i], turned[i] = (
                    rows[i] - (m_real[i] * rows[j] + m_imag[i] * turned[j]),
                    turned[i] - (m_real[i] * turned[j] - m_imag[i] * rows[j]),
                )
            for u in range(v + 1 if last else v, 4):
                x, y = col_real[u][j], col_imag[u][j]
                for l in below:
                    col_real[u][l] = col_real[u][l] - (x * m_real[l] + y * m_imag[l])
                    col_imag[u][l] = col_imag[u][l] - (y * m_real[l] - x * m_imag[l])
        for u in range(v, 4):
            new_a, new_b = a[u], b[u]
            if u > v or not last:
                for j in range(WIDTH):
                    x, y = col_real[u][j], col_imag[u][j]
                    row, row_turned = rows[j] * over[j], turned[j] * over[j]
                    new_a = new_a - (x * row + y * row_turned)
                    new_b = new_b - (x * row_turned - y * row)
                if u == v and s > 0:
                    new_a = jnp.where(sub < s, a[u], new_a)
                    new_b = jnp.where(sub < s, b[u], new_b)
            if u == v:
                for j in range(WIDTH):
                    new_a = jnp.where(sub == s + j, rows[j], new_a)
                    new_b = jnp.where(sub == s + j, turned[j], new_b)
            a[u], b[u] = new_a, new_b
    return [a[u] * (1.0 / jnp.sqrt(pivots[u])) for u in range(4)]


def wait_bytes(ref, sem):
    pltpu.make_async_copy(ref, ref, sem).wait()


def gram_kernel(
    bins_ref, weights_ref, snap_ref, parts_ref, lower_ref, upper_ref,
    bins_here, weights_here, x_ref, band_ref, sums_ref, gram_ref, pack_ref, got_s, half_ref, got_x, got_p,
    small_sem, in_sem, s_sems, x_sems, p_sems, l_sems, c_sems, r_sems,
):
    x, share, core = place()
    sibling = (x, share * 2 + 1 - core)
    smalls = [
        pltpu.make_async_copy(bins_ref, bins_here, small_sem.at[0]),
        pltpu.make_async_copy(weights_ref, weights_here, small_sem.at[1]),
    ]
    for small in smalls:
        small.start()
    loads = []
    for chunk in range(CHUNKS):
        load = pltpu.make_async_copy(snap_ref.at[chunk * CHUNK : (chunk + 1) * CHUNK, :], x_ref.at[chunk], in_sem.at[chunk])
        load.start()
        loads.append(load)

    def send(src, dst, sems, device):
        pltpu.make_async_remote_copy(
            src_ref=src, dst_ref=dst, send_sem=sems.at[0], recv_sem=sems.at[1], device_id=device, device_id_type=MESH
        ).start()

    barrier = pltpu.get_barrier_semaphore()
    pl.semaphore_signal(barrier, inc=1, device_id=sibling, device_id_type=MESH)
    for step in ROW_STEPS:
        pl.semaphore_signal(barrier, inc=1, device_id=row_peer(x, share, core, step)[1], device_id_type=MESH)
    for step in PLANE_STEPS:
        pl.semaphore_signal(barrier, inc=1, device_id=plane_peer(x, share, core, step)[1], device_id_type=MESH)

    for small in smalls:
        small.wait()
    build_band(bins_here, band_ref, sums_ref)
    for chunk in range(CHUNKS):
        loads[chunk].wait()
        transform_chunk(chunk, weights_here, x_ref, band_ref, sums_ref, parts_ref)
        add_gram(parts_ref, gram_ref, chunk)
    for f in range(FREQ):
        pack_ref[f % 2, f // 2] = packed_gram(gram_ref, f)
    pl.semaphore_wait(barrier, 1 + ROW - 1 + SHARES - 1)

    send(pack_ref.at[1 - core], got_s, s_sems, sibling)
    wait_bytes(got_s, s_sems.at[1])
    half_ref[...] = pack_ref[core] + got_s[...]

    for step in ROW_STEPS:
        other, device = row_peer(x, share, core, step)
        send(half_ref.at[other], got_x.at[x], x_sems, device)
    got_x[x] = half_ref[x]
    wait_bytes(got_x.at[0 : ROW - 1], x_sems.at[1])
    got_p[share] = (got_x[0] + got_x[1]) + (got_x[2] + got_x[3])

    for step in PLANE_STEPS:
        other, device = plane_peer(x, share, core, step)
        send(got_p.at[share], got_p.at[share], p_sems, device)
    wait_bytes(got_p.at[0 : SHARES - 1], p_sems.at[1])
    terms = [got_p[n] for n in range(SHARES)]
    while len(terms) > 1:
        terms = [terms[n] + terms[n + 1] for n in range(0, len(terms), 2)]

    rows = eliminate(terms[0])
    lane = lax.broadcasted_iota(jnp.int32, (8, 128), 1)
    for h in range(2):
        even, odd = rows[2 * h], rows[2 * h + 1]
        odd_far = pltpu.roll(odd, 64, 1)
        lower_ref[core, x, h] = jnp.where(lane < 64, odd_far, even)
        upper_ref[core, h] = jnp.where(lane < 64, even, odd_far)
    mine = lower_ref.at[core, x]
    for step in ROW_STEPS:
        other, device = row_peer(x, share, core, step)
        send(mine, mine, l_sems, device)
    send(upper_ref.at[core], upper_ref.at[core], r_sems, sibling)
    wait_bytes(lower_ref.at[0, 0 : ROW - 1], l_sems.at[1])
    send(lower_ref.at[core], lower_ref.at[core], c_sems, sibling)
    wait_bytes(lower_ref.at[0], c_sems.at[1])
    wait_bytes(upper_ref.at[0], r_sems.at[1])

    wait_bytes(got_s, s_sems.at[0])
    wait_bytes(got_x.at[0 : ROW - 1], x_sems.at[0])
    wait_bytes(got_p.at[0 : SHARES - 1], p_sems.at[0])
    wait_bytes(lower_ref.at[0, 0 : ROW - 1], l_sems.at[0])
    wait_bytes(lower_ref.at[0], c_sems.at[0])
    wait_bytes(upper_ref.at[0], r_sems.at[0])


def modes_kernel(parts_ref, lower_ref, packed_ref, modes_ref, upper_ref, out_ref, up_ref, out_sem, up_sem):
    i = lax.broadcasted_iota(jnp.int32, (NB, NB), 0)
    j = lax.broadcasted_iota(jnp.int32, (NB, NB), 1)
    for n in range(2):
        both = jnp.concatenate(
            [packed_ref[n, 0][:, :64], packed_ref[n, 0][:, 64:], packed_ref[n, 1][:, :64], packed_ref[n, 1][:, 64:]], axis=0
        )
        up_ref[0, n] = jnp.where(j >= i, both[:, :32], 0.0)
        up_ref[1, n] = jnp.where(j > i, both[:, 32:], 0.0)
    up_store = pltpu.make_async_copy(up_ref, upper_ref, up_sem)
    up_store.start()
    stores = []
    for f in range(FREQ):
        low, high = lower_ref[f % 2, f // 2, 0], lower_ref[f % 2, f // 2, 1]
        inv = jnp.concatenate([low[:, 64:], low[:, :64], high[:, 64:], high[:, :64]], axis=0) * math.sqrt(POINTS)
        inv = jnp.concatenate([inv, jnp.concatenate([-inv[:, 32:], inv[:, :32]], axis=1)], axis=0)
        hi = inv.astype(BF16)
        lo = (inv - hi.astype(F32)).astype(BF16)
        left = jnp.concatenate([hi, hi, lo], axis=1)
        modes = jnp.dot(left, parts_ref[f], preferred_element_type=F32)
        out_ref[0, f] = modes[0:32]
        out_ref[1, f] = modes[32:64]
        store = pltpu.make_async_copy(out_ref.at[:, f], modes_ref.at[:, f], out_sem.at[f])
        store.start()
        stores.append(store)
    up_store.wait()
    for store in stores:
        store.wait()


def body(snapshots, weights, freq_bins):
    dma = pltpu.SemaphoreType.DMA
    hbm = pl.BlockSpec(memory_space=pltpu.HBM)
    vmem = pl.BlockSpec(memory_space=pltpu.VMEM)
    snapshots, weights, freq_bins = (pltpu.with_memory_space_constraint(a, pltpu.HBM) for a in (snapshots, weights.reshape(8, 128), freq_bins))
    parts, lower, upper = pl.pallas_call(
        gram_kernel,
        out_shape=(
            jax.ShapeDtypeStruct((FREQ, 192, LOCAL), BF16),
            jax.ShapeDtypeStruct((2, ROW, 2, 8, 128), F32),
            jax.ShapeDtypeStruct((2, 2, 8, 128), F32),
        ),
        in_specs=[hbm, hbm, hbm],
        out_specs=(vmem, vmem, vmem),
        scratch_shapes=[
            pltpu.SMEM((FREQ,), jnp.int32),
            pltpu.VMEM((8, 128), F32),
            pltpu.VMEM((CHUNKS, CHUNK, SAMPLES), BF16),
            pltpu.VMEM((ROWS, BAND), BF16),
            pltpu.VMEM((128, 128), F32),
            pltpu.VMEM((FREQ, 64, 64), F32),
            pltpu.VMEM((2, ROW, 8, 128), F32),
            pltpu.VMEM((ROW, 8, 128), F32),
            pltpu.VMEM((ROW, 8, 128), F32),
            pltpu.VMEM((ROW, 8, 128), F32),
            pltpu.VMEM((SHARES, 8, 128), F32),
            dma((2,)), dma((CHUNKS,)),
            dma((2,)), dma((2,)), dma((2,)), dma((2,)), dma((2,)), dma((2,)),
        ],
        compiler_params=pltpu.CompilerParams(
            collective_id=0, has_side_effects=True, vmem_limit_bytes=GRAM_MIB * 1024 * 1024
        ),
        cost_estimate=pl.CostEstimate(flops=2_000_000_000, bytes_accessed=11_000_000, transcendentals=0),
    )(freq_bins, weights, snapshots)
    return pl.pallas_call(
        modes_kernel,
        out_shape=(
            jax.ShapeDtypeStruct((2, FREQ, NB, LOCAL), F32),
            jax.ShapeDtypeStruct((2, 2, NB, NB), F32),
        ),
        in_specs=[vmem, vmem, vmem],
        out_specs=(hbm, hbm),
        scratch_shapes=[
            pltpu.VMEM((2, FREQ, NB, LOCAL), F32),
            pltpu.VMEM((2, 2, NB, NB), F32),
            dma((FREQ,)), dma,
        ],
        compiler_params=pltpu.CompilerParams(vmem_limit_bytes=MODES_MIB * 1024 * 1024),
        cost_estimate=pl.CostEstimate(flops=400_000_000, bytes_accessed=5_000_000, transcendentals=0),
    )(parts, lower, upper)


def solution(mesh):
    return jax.shard_map(
        body,
        mesh=mesh,
        in_specs=(P(("freq", "pts"), None), P(("freq", "pts")), P()),
        out_specs=(P(None, None, None, ("freq", "pts")), P(None, "freq", None, None)),
        check_vma=False,
    )
```

```python
import math

import jax
import jax.numpy as jnp
from jax import lax
from jax.experimental import pallas as pl
from jax.experimental.pallas import tpu as pltpu
from jax.sharding import PartitionSpec as P

FREQ = 8
NB = 32
NFFT = 256
HALF = NFFT // 2
SAMPLES = 4224
POINTS = 131072
LOCAL = 1024
CHUNK = 256
CHUNKS = LOCAL // CHUNK
GROUPS = 4
BAND = 9 * HALF
ROWS = 144
ROW = 4
SHARES = 16
WIDTH = 4
GRAM_MIB = 44
MODES_MIB = 40
ROW_STEPS = (2, 1, 3)
PLANE_STEPS = (10, 6, 9, 11, 14, 2, 5, 7, 8, 13, 15, 1, 3, 4, 12)
MESH = pl.DeviceIdType.MESH
F32 = jnp.float32
BF16 = jnp.bfloat16
NT = (((1,), (1,)), ((), ()))


def place():
    x = lax.axis_index("freq")
    q = lax.axis_index("pts")
    return x, lax.div(q, 2), lax.rem(q, 2)


def row_peer(x, share, core, step):
    other = lax.rem(x + step, ROW)
    return other, (other, share * 2 + core)


def plane_peer(x, share, core, step):
    z, y = lax.div(share, 4), lax.rem(share, 4)
    other = lax.rem(z + step // 4, 4) * 4 + lax.rem(y + step % 4, 4)
    return other, (x, other * 2 + core)


def build_band(bins_ref, band_ref, sums_ref):
    row = lax.broadcasted_iota(jnp.int32, (FREQ, NFFT), 0)
    moment = lax.broadcasted_iota(jnp.int32, (FREQ, NFFT), 1)
    bins = jnp.zeros((FREQ, NFFT), jnp.int32)
    for f in range(FREQ):
        bins = jnp.where(row == f, bins_ref[f], bins)
    angle = lax.bitwise_and(bins * moment, NFFT - 1).astype(F32) * (2.0 * math.pi / NFFT)
    window = 0.5 - 0.5 * jnp.cos(moment.astype(F32) * (2.0 * math.pi / NFFT))
    cosine = (window * jnp.cos(angle)).astype(BF16).astype(F32)
    sine = (-window * jnp.sin(angle)).astype(BF16).astype(F32)
    slot = lax.broadcasted_iota(jnp.int32, (8, HALF), 0)
    for q in range(9):
        tiles = []
        for c in range(2 * FREQ):
            table = cosine if c < FREQ else sine
            line = table[c % FREQ : c % FREQ + 1]
            front = jnp.broadcast_to(line[:, :HALF], (8, HALF))
            back = jnp.broadcast_to(line[:, HALF:], (8, HALF))
            tiles.append(jnp.where(slot == q, front, jnp.where(slot == q - 1, back, 0.0)))
        mark = 0 if q < 8 else 1
        tiles.append(jnp.where(slot == mark, 1.0, 0.0))
        tiles.append(jnp.zeros((8, HALF), F32))
        band_ref[:, q * HALF : (q + 1) * HALF] = jnp.concatenate(tiles, axis=0).astype(BF16)
    ones = jnp.ones((BAND, 128), BF16)
    sums_ref[...] = jnp.dot(band_ref[0:128, :], ones, preferred_element_type=F32)


def transform_chunk(chunk, weights_ref, x_ref, band_ref, sums_ref, parts_ref):
    band = band_ref[...]
    groups = []
    total = jnp.zeros((1, CHUNK), F32)
    for g in range(GROUPS):
        x = x_ref[chunk, :, g * 8 * HALF : g * 8 * HALF + BAND]
        d = lax.dot_general(band, x, NT, preferred_element_type=F32)
        groups.append(d)
        total = total + d[128:129]
        if g == GROUPS - 1:
            total = total + d[129:130]
    mean = total * (1.0 / SAMPLES)
    w = jnp.concatenate([weights_ref[2 * chunk : 2 * chunk + 1], weights_ref[2 * chunk + 1 : 2 * chunk + 2]], axis=1)
    scale = jnp.sqrt(w * (1.0 / POINTS)) * (1.0 / math.sqrt(NB * 0.375 * NFFT))
    cols = slice(chunk * CHUNK, (chunk + 1) * CHUNK)
    for f in range(FREQ):
        for part in range(2):
            c = part * FREQ + f
            sums = sums_ref[c * 8 : c * 8 + 8, :]
            away = jnp.concatenate([sums, sums], axis=1) * mean
            y = jnp.concatenate([(d[c * 8 : c * 8 + 8] - away) * scale for d in groups], axis=0)
            hi = y.astype(BF16)
            lo = (y - hi.astype(F32)).astype(BF16)
            parts_ref[f, part * NB : (part + 1) * NB, cols] = hi
            parts_ref[f, 64 + part * NB : 64 + (part + 1) * NB, cols] = lo
            parts_ref[f, 128 + part * NB : 128 + (part + 1) * NB, cols] = hi


def add_gram(parts_ref, gram_ref, chunk):
    cols = slice(chunk * CHUNK, (chunk + 1) * CHUNK)
    for f in range(FREQ):
        both = parts_ref[f, 0:128, cols]
        s = lax.dot_general(both, both, NT, preferred_element_type=F32)
        s = s[0:64] + s[64:128]
        gram_ref[f] = s if chunk == 0 else gram_ref[f] + s


def packed_gram(gram_ref, f):
    s = gram_ref[f]
    s = s[:, 0:64] + s[:, 64:128]
    gram_real = s[0:32, 0:32] + s[32:64, 32:64]
    gram_imag = s[0:32, 32:64] - s[32:64, 0:32]
    i = lax.broadcasted_iota(jnp.int32, (NB, NB), 0)
    j = lax.broadcasted_iota(jnp.int32, (NB, NB), 1)
    packed = jnp.where(i >= j, gram_real, gram_imag)
    return jnp.concatenate([packed[8 * r : 8 * r + 8] for r in range(4)], axis=1)


def lanes(tile, k):
    return jnp.broadcast_to(tile[:, k : k + 1], (8, 128))


def sublanes(tile, s):
    return jnp.broadcast_to(tile[s : s + 1], (8, 128))


def unpack_gram(packed):
    p = jnp.concatenate([packed[:, 32 * r : 32 * r + 32] for r in range(4)], axis=0)
    t = p.T
    i = lax.broadcasted_iota(jnp.int32, (NB, NB), 0)
    j = lax.broadcasted_iota(jnp.int32, (NB, NB), 1)
    real = jnp.where(i >= j, p, t)
    imag = jnp.where(i < j, p, jnp.where(i > j, -t, 0.0))
    eye = jnp.where(i == j, 1.0, 0.0)
    zero = jnp.zeros((NB, NB), F32)
    whole = jnp.concatenate([real, imag, eye, zero], axis=1)
    turned = jnp.concatenate([-imag, real, zero, eye], axis=1)
    return [whole[8 * u : 8 * u + 8] for u in range(4)], [turned[8 * u : 8 * u + 8] for u in range(4)]


def eliminate_panel(a, b, pivots, first):
    sub = lax.broadcasted_iota(jnp.int32, (8, 128), 0)
    v, s = first // 8, first % 8
    last = s + WIDTH == 8
    col_real = {u: [lanes(a[u], first + j) for j in range(WIDTH)] for u in range(v, 4)}
    col_imag = {u: [lanes(a[u], NB + first + j) for j in range(WIDTH)] for u in range(v, 4)}
    rows = [sublanes(a[v], s + j) for j in range(WIDTH)]
    turned = [sublanes(b[v], s + j) for j in range(WIDTH)]
    block_real = [[sublanes(col_real[v][l], s + i) for l in range(i + 1)] for i in range(WIDTH)]
    block_imag = [[sublanes(col_imag[v][l], s + i) for l in range(i)] for i in range(WIDTH)]
    over = []
    for j in range(WIDTH):
        pivot = block_real[j][j]
        inverse = 1.0 / pivot
        over.append(inverse)
        pivots[v] = jnp.where(sub == s + j, pivot, pivots[v])
        below = range(j + 1, WIDTH)
        m_real = {i: block_real[i][j] * inverse for i in below}
        m_imag = {i: block_imag[i][j] * inverse for i in below}
        for i in below:
            for l in range(j + 1, i + 1):
                other_real, other_imag = block_real[l][j], block_imag[l][j]
                block_real[i][l] = block_real[i][l] - (m_real[i] * other_real + m_imag[i] * other_imag)
                if l < i:
                    block_imag[i][l] = block_imag[i][l] - (m_imag[i] * other_real - m_real[i] * other_imag)
        for i in below:
            rows[i], turned[i] = (
                rows[i] - (m_real[i] * rows[j] + m_imag[i] * turned[j]),
                turned[i] - (m_real[i] * turned[j] - m_imag[i] * rows[j]),
            )
        for u in range(v + 1 if last else v, 4):
            x, y = col_real[u][j], col_imag[u][j]
            for l in below:
                col_real[u][l] = col_real[u][l] - (x * m_real[l] + y * m_imag[l])
                col_imag[u][l] = col_imag[u][l] - (y * m_real[l] - x * m_imag[l])
    for u in range(v, 4):
        new_a, new_b = a[u], b[u]
        if u > v or not last:
            for j in range(WIDTH):
                x, y = col_real[u][j], col_imag[u][j]
                row, row_turned = rows[j] * over[j], turned[j] * over[j]
                new_a = new_a - (x * row + y * row_turned)
                new_b = new_b - (x * row_turned - y * row)
            if u == v and s > 0:
                new_a = jnp.where(sub < s, a[u], new_a)
                new_b = jnp.where(sub < s, b[u], new_b)
        if u == v:
            for j in range(WIDTH):
                new_a = jnp.where(sub == s + j, rows[j], new_a)
                new_b = jnp.where(sub == s + j, turned[j], new_b)
        a[u], b[u] = new_a, new_b


def eliminate(packs):
    states = [unpack_gram(packed) for packed in packs]
    pivots = [[jnp.ones((8, 128), F32) for _ in range(4)] for _ in packs]
    for first in range(0, NB, WIDTH):
        for (a, b), pivot in zip(states, pivots):
            eliminate_panel(a, b, pivot, first)
    return [[a[u] * (1.0 / jnp.sqrt(pivot[u])) for u in range(4)] for (a, b), pivot in zip(states, pivots)]


def wait_bytes(ref, sem):
    pltpu.make_async_copy(ref, ref, sem).wait()


def gram_kernel(
    bins_ref, weights_ref, snap_ref, parts_ref, lower_ref, upper_ref,
    bins_here, weights_here, x_ref, band_ref, sums_ref, gram_ref, pack_ref, got_s, got_x, got_p, all_upper,
    small_sem, in_sem, s_sems, x_sems, p_sems, c_sems, r_sems,
):
    x, share, core = place()
    sibling = (x, share * 2 + 1 - core)
    smalls = [
        pltpu.make_async_copy(bins_ref, bins_here, small_sem.at[0]),
        pltpu.make_async_copy(weights_ref, weights_here, small_sem.at[1]),
    ]
    for small in smalls:
        small.start()
    loads = []
    for chunk in range(CHUNKS):
        load = pltpu.make_async_copy(snap_ref.at[chunk * CHUNK : (chunk + 1) * CHUNK, :], x_ref.at[chunk], in_sem.at[chunk])
        load.start()
        loads.append(load)

    def send(src, dst, sems, device):
        pltpu.make_async_remote_copy(
            src_ref=src, dst_ref=dst, send_sem=sems.at[0], recv_sem=sems.at[1], device_id=device, device_id_type=MESH
        ).start()

    barrier = pltpu.get_barrier_semaphore()
    pl.semaphore_signal(barrier, inc=1, device_id=sibling, device_id_type=MESH)
    for step in ROW_STEPS:
        pl.semaphore_signal(barrier, inc=1, device_id=row_peer(x, share, core, step)[1], device_id_type=MESH)
    for step in PLANE_STEPS:
        pl.semaphore_signal(barrier, inc=1, device_id=plane_peer(x, share, core, step)[1], device_id_type=MESH)

    for small in smalls:
        small.wait()
    build_band(bins_here, band_ref, sums_ref)
    for chunk in range(CHUNKS):
        loads[chunk].wait()
        transform_chunk(chunk, weights_here, x_ref, band_ref, sums_ref, parts_ref)
        if chunk > 0:
            add_gram(parts_ref, gram_ref, chunk - 1)
    add_gram(parts_ref, gram_ref, CHUNKS - 1)
    for f in range(FREQ):
        pack_ref[f % 2, f // 2] = packed_gram(gram_ref, f)
    pl.semaphore_wait(barrier, 1 + ROW - 1 + SHARES - 1)

    send(pack_ref.at[1 - core], got_s, s_sems, sibling)
    wait_bytes(got_s, s_sems.at[1])
    got_x[x] = pack_ref[core] + got_s[...]

    for step in ROW_STEPS:
        send(got_x.at[x], got_x.at[x], x_sems, row_peer(x, share, core, step)[1])
    wait_bytes(got_x.at[0 : ROW - 1], x_sems.at[1])
    got_p[share] = (got_x[0] + got_x[1]) + (got_x[2] + got_x[3])

    for step in PLANE_STEPS:
        send(got_p.at[share], got_p.at[share], p_sems, plane_peer(x, share, core, step)[1])
    wait_bytes(got_p.at[0 : SHARES - 1], p_sems.at[1])
    packs = []
    for n in range(FREQ // 2):
        terms = [got_p[m, n] for m in range(SHARES)]
        while len(terms) > 1:
            terms = [terms[m] + terms[m + 1] for m in range(0, len(terms), 2)]
        packs.append(terms[0])

    lane = lax.broadcasted_iota(jnp.int32, (8, 128), 1)
    for n, rows in enumerate(eliminate(packs)):
        for h in range(2):
            even, odd = rows[2 * h], rows[2 * h + 1]
            odd_far = pltpu.roll(odd, 64, 1)
            lower_ref[core, n, h] = jnp.where(lane < 64, odd_far, even)
            all_upper[n, h] = jnp.where(lane < 64, even, odd_far)
    send(lower_ref.at[core], lower_ref.at[core], c_sems, sibling)
    upper_ref[core] = all_upper[x]
    send(upper_ref.at[core], upper_ref.at[core], r_sems, sibling)
    wait_bytes(lower_ref.at[0], c_sems.at[1])
    wait_bytes(upper_ref.at[0], r_sems.at[1])

    wait_bytes(got_s, s_sems.at[0])
    wait_bytes(got_x.at[0 : ROW - 1], x_sems.at[0])
    wait_bytes(got_p.at[0 : SHARES - 1], p_sems.at[0])
    wait_bytes(lower_ref.at[0], c_sems.at[0])
    wait_bytes(upper_ref.at[0], r_sems.at[0])


def modes_kernel(parts_ref, lower_ref, packed_ref, modes_ref, upper_ref, out_ref, up_ref, out_sem, up_sem):
    i = lax.broadcasted_iota(jnp.int32, (NB, NB), 0)
    j = lax.broadcasted_iota(jnp.int32, (NB, NB), 1)
    for n in range(2):
        both = jnp.concatenate(
            [packed_ref[n, 0][:, :64], packed_ref[n, 0][:, 64:], packed_ref[n, 1][:, :64], packed_ref[n, 1][:, 64:]], axis=0
        )
        up_ref[0, n] = jnp.where(j >= i, both[:, :32], 0.0)
        up_ref[1, n] = jnp.where(j > i, both[:, 32:], 0.0)
    up_store = pltpu.make_async_copy(up_ref, upper_ref, up_sem)
    up_store.start()
    stores = []
    for f in range(FREQ):
        low, high = lower_ref[f % 2, f // 2, 0], lower_ref[f % 2, f // 2, 1]
        inv = jnp.concatenate([low[:, 64:], low[:, :64], high[:, 64:], high[:, :64]], axis=0) * math.sqrt(POINTS)
        inv = jnp.concatenate([inv, jnp.concatenate([-inv[:, 32:], inv[:, :32]], axis=1)], axis=0)
        hi = inv.astype(BF16)
        lo = (inv - hi.astype(F32)).astype(BF16)
        left = jnp.concatenate([hi, hi, lo], axis=1)
        modes = jnp.dot(left, parts_ref[f], preferred_element_type=F32)
        out_ref[0, f] = modes[0:32]
        out_ref[1, f] = modes[32:64]
        store = pltpu.make_async_copy(out_ref.at[:, f], modes_ref.at[:, f], out_sem.at[f])
        store.start()
        stores.append(store)
    up_store.wait()
    for store in stores:
        store.wait()


def body(snapshots, weights, freq_bins):
    dma = pltpu.SemaphoreType.DMA
    hbm = pl.BlockSpec(memory_space=pltpu.HBM)
    vmem = pl.BlockSpec(memory_space=pltpu.VMEM)
    snapshots, weights, freq_bins = (pltpu.with_memory_space_constraint(a, pltpu.HBM) for a in (snapshots, weights.reshape(8, 128), freq_bins))
    parts, lower, upper = pl.pallas_call(
        gram_kernel,
        out_shape=(
            jax.ShapeDtypeStruct((FREQ, 192, LOCAL), BF16),
            jax.ShapeDtypeStruct((2, ROW, 2, 8, 128), F32),
            jax.ShapeDtypeStruct((2, 2, 8, 128), F32),
        ),
        in_specs=[hbm, hbm, hbm],
        out_specs=(vmem, vmem, vmem),
        scratch_shapes=[
            pltpu.SMEM((FREQ,), jnp.int32),
            pltpu.VMEM((8, 128), F32),
            pltpu.VMEM((CHUNKS, CHUNK, SAMPLES), BF16),
            pltpu.VMEM((ROWS, BAND), BF16),
            pltpu.VMEM((128, 128), F32),
            pltpu.VMEM((FREQ, 64, 128), F32),
            pltpu.VMEM((2, ROW, 8, 128), F32),
            pltpu.VMEM((ROW, 8, 128), F32),
            pltpu.VMEM((ROW, ROW, 8, 128), F32),
            pltpu.VMEM((SHARES, ROW, 8, 128), F32),
            pltpu.VMEM((ROW, 2, 8, 128), F32),
            dma((2,)), dma((CHUNKS,)),
            dma((2,)), dma((2,)), dma((2,)), dma((2,)), dma((2,)),
        ],
        compiler_params=pltpu.CompilerParams(
            collective_id=0, has_side_effects=True, vmem_limit_bytes=GRAM_MIB * 1024 * 1024
        ),
        cost_estimate=pl.CostEstimate(flops=2_000_000_000, bytes_accessed=11_000_000, transcendentals=0),
    )(freq_bins, weights, snapshots)
    return pl.pallas_call(
        modes_kernel,
        out_shape=(
            jax.ShapeDtypeStruct((2, FREQ, NB, LOCAL), F32),
            jax.ShapeDtypeStruct((2, 2, NB, NB), F32),
        ),
        in_specs=[vmem, vmem, vmem],
        out_specs=(hbm, hbm),
        scratch_shapes=[
            pltpu.VMEM((2, FREQ, NB, LOCAL), F32),
            pltpu.VMEM((2, 2, NB, NB), F32),
            dma((FREQ,)), dma,
        ],
        compiler_params=pltpu.CompilerParams(vmem_limit_bytes=MODES_MIB * 1024 * 1024),
        cost_estimate=pl.CostEstimate(flops=400_000_000, bytes_accessed=5_000_000, transcendentals=0),
    )(parts, lower, upper)


def solution(mesh):
    return jax.shard_map(
        body,
        mesh=mesh,
        in_specs=(P(("freq", "pts"), None), P(("freq", "pts")), P()),
        out_specs=(P(None, None, None, ("freq", "pts")), P(None, "freq", None, None)),
        check_vma=False,
    )
```

```python
import math

import jax
import jax.numpy as jnp
from jax import lax
from jax.experimental import pallas as pl
from jax.experimental.pallas import tpu as pltpu
from jax.sharding import PartitionSpec as P

FREQ = 8
NB = 32
NFFT = 256
HALF = NFFT // 2
SAMPLES = 4224
POINTS = 131072
LOCAL = 1024
CHUNK = 256
CHUNKS = LOCAL // CHUNK
GROUPS = 4
BAND = 9 * HALF
ROWS = 144
ROW = 4
SHARES = 16
WIDTH = 4
GRAM_MIB = 44
MODES_MIB = 40
ROW_STEPS = (2, 1, 3)
PLANE_STEPS = (10, 6, 9, 11, 14, 2, 5, 7, 8, 13, 15, 1, 3, 4, 12)
MESH = pl.DeviceIdType.MESH
F32 = jnp.float32
BF16 = jnp.bfloat16
NT = (((1,), (1,)), ((), ()))


def place():
    x = lax.axis_index("freq")
    q = lax.axis_index("pts")
    return x, lax.div(q, 2), lax.rem(q, 2)


def row_peer(x, share, core, step):
    other = lax.rem(x + step, ROW)
    return other, (other, share * 2 + core)


def plane_peer(x, share, core, step):
    z, y = lax.div(share, 4), lax.rem(share, 4)
    other = lax.rem(z + step // 4, 4) * 4 + lax.rem(y + step % 4, 4)
    return other, (x, other * 2 + core)


def build_band(bins_ref, band_ref, sums_ref):
    row = lax.broadcasted_iota(jnp.int32, (FREQ, NFFT), 0)
    moment = lax.broadcasted_iota(jnp.int32, (FREQ, NFFT), 1)
    bins = jnp.zeros((FREQ, NFFT), jnp.int32)
    for f in range(FREQ):
        bins = jnp.where(row == f, bins_ref[f], bins)
    angle = lax.bitwise_and(bins * moment, NFFT - 1).astype(F32) * (2.0 * math.pi / NFFT)
    window = 0.5 - 0.5 * jnp.cos(moment.astype(F32) * (2.0 * math.pi / NFFT))
    cosine = (window * jnp.cos(angle)).astype(BF16).astype(F32)
    sine = (-window * jnp.sin(angle)).astype(BF16).astype(F32)
    slot = lax.broadcasted_iota(jnp.int32, (8, HALF), 0)
    for q in range(9):
        tiles = []
        for c in range(2 * FREQ):
            table = cosine if c < FREQ else sine
            line = table[c % FREQ : c % FREQ + 1]
            front = jnp.broadcast_to(line[:, :HALF], (8, HALF))
            back = jnp.broadcast_to(line[:, HALF:], (8, HALF))
            tiles.append(jnp.where(slot == q, front, jnp.where(slot == q - 1, back, 0.0)))
        mark = 0 if q < 8 else 1
        tiles.append(jnp.where(slot == mark, 1.0, 0.0))
        tiles.append(jnp.zeros((8, HALF), F32))
        band_ref[:, q * HALF : (q + 1) * HALF] = jnp.concatenate(tiles, axis=0).astype(BF16)
    ones = jnp.ones((BAND, 128), BF16)
    sums_ref[...] = jnp.dot(band_ref[0:128, :], ones, preferred_element_type=F32)


def multiply_chunk(chunk, x_ref, band_ref, held_ref):
    band = band_ref[...]
    for g in range(GROUPS):
        x = x_ref[chunk, :, g * 8 * HALF : g * 8 * HALF + BAND]
        held_ref[chunk % 2, g] = lax.dot_general(band, x, NT, preferred_element_type=F32)


def finish_chunk(chunk, weights_ref, held_ref, sums_ref, parts_ref):
    held = held_ref.at[chunk % 2]
    total = held[GROUPS - 1, 129:130, :]
    for g in range(GROUPS):
        total = total + held[g, 128:129, :]
    mean = total * (1.0 / SAMPLES)
    w = jnp.concatenate([weights_ref[2 * chunk : 2 * chunk + 1], weights_ref[2 * chunk + 1 : 2 * chunk + 2]], axis=1)
    scale = jnp.sqrt(w * (1.0 / POINTS)) * (1.0 / math.sqrt(NB * 0.375 * NFFT))
    cols = slice(chunk * CHUNK, (chunk + 1) * CHUNK)
    for f in range(FREQ):
        for part in range(2):
            c = part * FREQ + f
            sums = sums_ref[c * 8 : c * 8 + 8, :]
            away = jnp.concatenate([sums, sums], axis=1) * mean
            y = jnp.concatenate([(held[g, c * 8 : c * 8 + 8, :] - away) * scale for g in range(GROUPS)], axis=0)
            hi = y.astype(BF16)
            lo = (y - hi.astype(F32)).astype(BF16)
            parts_ref[f, part * NB : (part + 1) * NB, cols] = hi
            parts_ref[f, 64 + part * NB : 64 + (part + 1) * NB, cols] = lo
            parts_ref[f, 128 + part * NB : 128 + (part + 1) * NB, cols] = hi


def add_gram(parts_ref, gram_ref, chunk):
    cols = slice(chunk * CHUNK, (chunk + 1) * CHUNK)
    for f in range(FREQ):
        both = parts_ref[f, 0:128, cols]
        s = lax.dot_general(both, both, NT, preferred_element_type=F32)
        s = s[0:64] + s[64:128]
        gram_ref[f] = s if chunk == 0 else gram_ref[f] + s


def packed_gram(gram_ref, f):
    s = gram_ref[f]
    s = s[:, 0:64] + s[:, 64:128]
    gram_real = s[0:32, 0:32] + s[32:64, 32:64]
    gram_imag = s[0:32, 32:64] - s[32:64, 0:32]
    i = lax.broadcasted_iota(jnp.int32, (NB, NB), 0)
    j = lax.broadcasted_iota(jnp.int32, (NB, NB), 1)
    packed = jnp.where(i >= j, gram_real, gram_imag)
    return jnp.concatenate([packed[8 * r : 8 * r + 8] for r in range(4)], axis=1)


def lanes(tile, k):
    return jnp.broadcast_to(tile[:, k : k + 1], (8, 128))


def sublanes(tile, s):
    return jnp.broadcast_to(tile[s : s + 1], (8, 128))


def unpack_gram(packed):
    p = jnp.concatenate([packed[:, 32 * r : 32 * r + 32] for r in range(4)], axis=0)
    t = p.T
    i = lax.broadcasted_iota(jnp.int32, (NB, NB), 0)
    j = lax.broadcasted_iota(jnp.int32, (NB, NB), 1)
    real = jnp.where(i >= j, p, t)
    imag = jnp.where(i < j, p, jnp.where(i > j, -t, 0.0))
    eye = jnp.where(i == j, 1.0, 0.0)
    zero = jnp.zeros((NB, NB), F32)
    whole = jnp.concatenate([real, imag, eye, zero], axis=1)
    turned = jnp.concatenate([-imag, real, zero, eye], axis=1)
    return [whole[8 * u : 8 * u + 8] for u in range(4)], [turned[8 * u : 8 * u + 8] for u in range(4)]


def eliminate_panel(a, b, pivots, first):
    sub = lax.broadcasted_iota(jnp.int32, (8, 128), 0)
    v, s = first // 8, first % 8
    last = s + WIDTH == 8
    col_real = {u: [lanes(a[u], first + j) for j in range(WIDTH)] for u in range(v, 4)}
    col_imag = {u: [lanes(a[u], NB + first + j) for j in range(WIDTH)] for u in range(v, 4)}
    rows = [sublanes(a[v], s + j) for j in range(WIDTH)]
    turned = [sublanes(b[v], s + j) for j in range(WIDTH)]
    block_real = [[sublanes(col_real[v][l], s + i) for l in range(i + 1)] for i in range(WIDTH)]
    block_imag = [[sublanes(col_imag[v][l], s + i) for l in range(i)] for i in range(WIDTH)]
    over = []
    for j in range(WIDTH):
        pivot = block_real[j][j]
        inverse = 1.0 / pivot
        over.append(inverse)
        pivots[v] = jnp.where(sub == s + j, pivot, pivots[v])
        below = range(j + 1, WIDTH)
        m_real = {i: block_real[i][j] * inverse for i in below}
        m_imag = {i: block_imag[i][j] * inverse for i in below}
        for i in below:
            for l in range(j + 1, i + 1):
                other_real, other_imag = block_real[l][j], block_imag[l][j]
                block_real[i][l] = block_real[i][l] - (m_real[i] * other_real + m_imag[i] * other_imag)
                if l < i:
                    block_imag[i][l] = block_imag[i][l] - (m_imag[i] * other_real - m_real[i] * other_imag)
        for i in below:
            rows[i], turned[i] = (
                rows[i] - (m_real[i] * rows[j] + m_imag[i] * turned[j]),
                turned[i] - (m_real[i] * turned[j] - m_imag[i] * rows[j]),
            )
        for u in range(v + 1 if last else v, 4):
            x, y = col_real[u][j], col_imag[u][j]
            for l in below:
                col_real[u][l] = col_real[u][l] - (x * m_real[l] + y * m_imag[l])
                col_imag[u][l] = col_imag[u][l] - (y * m_real[l] - x * m_imag[l])
    for u in range(v, 4):
        new_a, new_b = a[u], b[u]
        if u > v or not last:
            for j in range(WIDTH):
                x, y = col_real[u][j], col_imag[u][j]
                row, row_turned = rows[j] * over[j], turned[j] * over[j]
                new_a = new_a - (x * row + y * row_turned)
                new_b = new_b - (x * row_turned - y * row)
            if u == v and s > 0:
                new_a = jnp.where(sub < s, a[u], new_a)
                new_b = jnp.where(sub < s, b[u], new_b)
        if u == v:
            for j in range(WIDTH):
                new_a = jnp.where(sub == s + j, rows[j], new_a)
                new_b = jnp.where(sub == s + j, turned[j], new_b)
        a[u], b[u] = new_a, new_b


def eliminate(packs):
    states = [unpack_gram(packed) for packed in packs]
    pivots = [[jnp.ones((8, 128), F32) for _ in range(4)] for _ in packs]
    for first in range(0, NB, WIDTH):
        for (a, b), pivot in zip(states, pivots):
            eliminate_panel(a, b, pivot, first)
    return [[a[u] * (1.0 / jnp.sqrt(pivot[u])) for u in range(4)] for (a, b), pivot in zip(states, pivots)]


def wait_bytes(ref, sem):
    pltpu.make_async_copy(ref, ref, sem).wait()


def gram_kernel(
    bins_ref, weights_ref, snap_ref, parts_ref, lower_ref, upper_ref,
    bins_here, weights_here, x_ref, band_ref, sums_ref, held_ref, gram_ref, pack_ref, got_s, got_x, got_p, all_upper,
    small_sem, in_sem, s_sems, x_sems, p_sems, c_sems, r_sems,
):
    x, share, core = place()
    sibling = (x, share * 2 + 1 - core)
    def send(src, dst, sems, device):
        pltpu.make_async_remote_copy(
            src_ref=src, dst_ref=dst, send_sem=sems.at[0], recv_sem=sems.at[1], device_id=device, device_id_type=MESH
        ).start()

    barrier = pltpu.get_barrier_semaphore()

    def greet(device):
        pl.semaphore_signal(barrier, inc=1, device_id=device, device_id_type=MESH)

    smalls = [
        pltpu.make_async_copy(bins_ref, bins_here, small_sem.at[0]),
        pltpu.make_async_copy(weights_ref, weights_here, small_sem.at[1]),
    ]
    for small in smalls:
        small.start()
    loads = [
        pltpu.make_async_copy(snap_ref.at[chunk * CHUNK : (chunk + 1) * CHUNK, :], x_ref.at[chunk], in_sem.at[chunk])
        for chunk in range(CHUNKS)
    ]
    loads[0].start()
    for step in PLANE_STEPS[:8]:
        greet(plane_peer(x, share, core, step)[1])
    loads[1].start()
    for step in PLANE_STEPS[8:]:
        greet(plane_peer(x, share, core, step)[1])
    for load in loads[2:]:
        load.start()
    for small in smalls:
        small.wait()
    build_band(bins_here, band_ref, sums_ref)
    for step in ROW_STEPS:
        greet(row_peer(x, share, core, step)[1])
    greet(sibling)
    for chunk in range(CHUNKS):
        loads[chunk].wait()
        multiply_chunk(chunk, x_ref, band_ref, held_ref)
        if chunk > 0:
            finish_chunk(chunk - 1, weights_here, held_ref, sums_ref, parts_ref)
            add_gram(parts_ref, gram_ref, chunk - 1)
    finish_chunk(CHUNKS - 1, weights_here, held_ref, sums_ref, parts_ref)
    add_gram(parts_ref, gram_ref, CHUNKS - 1)
    for f in range(FREQ):
        pack_ref[f % 2, f // 2] = packed_gram(gram_ref, f)
    pl.semaphore_wait(barrier, 1 + ROW - 1 + SHARES - 1)

    send(pack_ref.at[1 - core], got_s, s_sems, sibling)
    wait_bytes(got_s, s_sems.at[1])
    got_x[x] = pack_ref[core] + got_s[...]

    for step in ROW_STEPS:
        send(got_x.at[x], got_x.at[x], x_sems, row_peer(x, share, core, step)[1])
    wait_bytes(got_x.at[0 : ROW - 1], x_sems.at[1])
    got_p[share] = (got_x[0] + got_x[1]) + (got_x[2] + got_x[3])

    for step in PLANE_STEPS:
        send(got_p.at[share], got_p.at[share], p_sems, plane_peer(x, share, core, step)[1])
    wait_bytes(got_p.at[0 : SHARES - 1], p_sems.at[1])
    packs = []
    for n in range(FREQ // 2):
        terms = [got_p[m, n] for m in range(SHARES)]
        while len(terms) > 1:
            terms = [terms[m] + terms[m + 1] for m in range(0, len(terms), 2)]
        packs.append(terms[0])

    lane = lax.broadcasted_iota(jnp.int32, (8, 128), 1)
    for n, rows in enumerate(eliminate(packs)):
        for h in range(2):
            even, odd = rows[2 * h], rows[2 * h + 1]
            odd_far = pltpu.roll(odd, 64, 1)
            lower_ref[core, n, h] = jnp.where(lane < 64, odd_far, even)
            all_upper[n, h] = jnp.where(lane < 64, even, odd_far)
    send(lower_ref.at[core], lower_ref.at[core], c_sems, sibling)
    upper_ref[core] = all_upper[x]
    send(upper_ref.at[core], upper_ref.at[core], r_sems, sibling)
    wait_bytes(lower_ref.at[0], c_sems.at[1])
    wait_bytes(upper_ref.at[0], r_sems.at[1])

    wait_bytes(got_s, s_sems.at[0])
    wait_bytes(got_x.at[0 : ROW - 1], x_sems.at[0])
    wait_bytes(got_p.at[0 : SHARES - 1], p_sems.at[0])
    wait_bytes(lower_ref.at[0], c_sems.at[0])
    wait_bytes(upper_ref.at[0], r_sems.at[0])


def modes_kernel(parts_ref, lower_ref, packed_ref, modes_ref, upper_ref, out_ref, up_ref, out_sem, up_sem):
    i = lax.broadcasted_iota(jnp.int32, (NB, NB), 0)
    j = lax.broadcasted_iota(jnp.int32, (NB, NB), 1)
    for n in range(2):
        both = jnp.concatenate(
            [packed_ref[n, 0][:, :64], packed_ref[n, 0][:, 64:], packed_ref[n, 1][:, :64], packed_ref[n, 1][:, 64:]], axis=0
        )
        up_ref[0, n] = jnp.where(j >= i, both[:, :32], 0.0)
        up_ref[1, n] = jnp.where(j > i, both[:, 32:], 0.0)
    up_store = pltpu.make_async_copy(up_ref, upper_ref, up_sem)
    up_store.start()
    stores = []
    for f in range(FREQ):
        low, high = lower_ref[f % 2, f // 2, 0], lower_ref[f % 2, f // 2, 1]
        inv = jnp.concatenate([low[:, 64:], low[:, :64], high[:, 64:], high[:, :64]], axis=0) * math.sqrt(POINTS)
        inv = jnp.concatenate([inv, jnp.concatenate([-inv[:, 32:], inv[:, :32]], axis=1)], axis=0)
        hi = inv.astype(BF16)
        lo = (inv - hi.astype(F32)).astype(BF16)
        left = jnp.concatenate([hi, hi, lo], axis=1)
        modes = jnp.dot(left, parts_ref[f], preferred_element_type=F32)
        out_ref[0, f] = modes[0:32]
        out_ref[1, f] = modes[32:64]
        store = pltpu.make_async_copy(out_ref.at[:, f], modes_ref.at[:, f], out_sem.at[f])
        store.start()
        stores.append(store)
    up_store.wait()
    for store in stores:
        store.wait()


def body(snapshots, weights, freq_bins):
    dma = pltpu.SemaphoreType.DMA
    hbm = pl.BlockSpec(memory_space=pltpu.HBM)
    vmem = pl.BlockSpec(memory_space=pltpu.VMEM)
    snapshots, weights, freq_bins = (pltpu.with_memory_space_constraint(a, pltpu.HBM) for a in (snapshots, weights.reshape(8, 128), freq_bins))
    parts, lower, upper = pl.pallas_call(
        gram_kernel,
        out_shape=(
            jax.ShapeDtypeStruct((FREQ, 192, LOCAL), BF16),
            jax.ShapeDtypeStruct((2, ROW, 2, 8, 128), F32),
            jax.ShapeDtypeStruct((2, 2, 8, 128), F32),
        ),
        in_specs=[hbm, hbm, hbm],
        out_specs=(vmem, vmem, vmem),
        scratch_shapes=[
            pltpu.SMEM((FREQ,), jnp.int32),
            pltpu.VMEM((8, 128), F32),
            pltpu.VMEM((CHUNKS, CHUNK, SAMPLES), BF16),
            pltpu.VMEM((ROWS, BAND), BF16),
            pltpu.VMEM((128, 128), F32),
            pltpu.VMEM((2, GROUPS, ROWS, CHUNK), F32),
            pltpu.VMEM((FREQ, 64, 128), F32),
            pltpu.VMEM((2, ROW, 8, 128), F32),
            pltpu.VMEM((ROW, 8, 128), F32),
            pltpu.VMEM((ROW, ROW, 8, 128), F32),
            pltpu.VMEM((SHARES, ROW, 8, 128), F32),
            pltpu.VMEM((ROW, 2, 8, 128), F32),
            dma((2,)), dma((CHUNKS,)),
            dma((2,)), dma((2,)), dma((2,)), dma((2,)), dma((2,)),
        ],
        compiler_params=pltpu.CompilerParams(
            collective_id=0, has_side_effects=True, vmem_limit_bytes=GRAM_MIB * 1024 * 1024
        ),
        cost_estimate=pl.CostEstimate(flops=2_000_000_000, bytes_accessed=11_000_000, transcendentals=0),
    )(freq_bins, weights, snapshots)
    return pl.pallas_call(
        modes_kernel,
        out_shape=(
            jax.ShapeDtypeStruct((2, FREQ, NB, LOCAL), F32),
            jax.ShapeDtypeStruct((2, 2, NB, NB), F32),
        ),
        in_specs=[vmem, vmem, vmem],
        out_specs=(hbm, hbm),
        scratch_shapes=[
            pltpu.VMEM((2, FREQ, NB, LOCAL), F32),
            pltpu.VMEM((2, 2, NB, NB), F32),
            dma((FREQ,)), dma,
        ],
        compiler_params=pltpu.CompilerParams(vmem_limit_bytes=MODES_MIB * 1024 * 1024),
        cost_estimate=pl.CostEstimate(flops=400_000_000, bytes_accessed=5_000_000, transcendentals=0),
    )(parts, lower, upper)


def solution(mesh):
    return jax.shard_map(
        body,
        mesh=mesh,
        in_specs=(P(("freq", "pts"), None), P(("freq", "pts")), P()),
        out_specs=(P(None, None, None, ("freq", "pts")), P(None, "freq", None, None)),
        check_vma=False,
    )
```

```python
import math

import jax
import jax.numpy as jnp
from jax import lax
from jax.experimental import pallas as pl
from jax.experimental.pallas import tpu as pltpu
from jax.sharding import PartitionSpec as P

FREQ = 8
NB = 32
NFFT = 256
HALF = NFFT // 2
SAMPLES = 4224
POINTS = 131072
LOCAL = 1024
CHUNK = 256
CHUNKS = LOCAL // CHUNK
GROUPS = 4
BAND = 9 * HALF
ROWS = 144
ROW = 4
SHARES = 16
WIDTH = 4
GRAM_MIB = 44
MODES_MIB = 40
ROW_STEPS = (2, 1, 3)
PLANE_STEPS = (10, 6, 9, 11, 14, 2, 5, 7, 8, 13, 15, 1, 3, 4, 12)
MESH = pl.DeviceIdType.MESH
F32 = jnp.float32
BF16 = jnp.bfloat16
NT = (((1,), (1,)), ((), ()))


def place():
    x = lax.axis_index("freq")
    q = lax.axis_index("pts")
    return x, lax.div(q, 2), lax.rem(q, 2)


def row_peer(x, share, core, step):
    other = lax.rem(x + step, ROW)
    return other, (other, share * 2 + core)


def plane_peer(x, share, core, step):
    z, y = lax.div(share, 4), lax.rem(share, 4)
    other = lax.rem(z + step // 4, 4) * 4 + lax.rem(y + step % 4, 4)
    return other, (x, other * 2 + core)


def build_band(bins_ref, band_ref, sums_ref):
    row = lax.broadcasted_iota(jnp.int32, (FREQ, NFFT), 0)
    moment = lax.broadcasted_iota(jnp.int32, (FREQ, NFFT), 1)
    bins = jnp.zeros((FREQ, NFFT), jnp.int32)
    for f in range(FREQ):
        bins = jnp.where(row == f, bins_ref[f], bins)
    angle = lax.bitwise_and(bins * moment, NFFT - 1).astype(F32) * (2.0 * math.pi / NFFT)
    window = 0.5 - 0.5 * jnp.cos(moment.astype(F32) * (2.0 * math.pi / NFFT))
    cosine = (window * jnp.cos(angle)).astype(BF16).astype(F32)
    sine = (-window * jnp.sin(angle)).astype(BF16).astype(F32)
    slot = lax.broadcasted_iota(jnp.int32, (8, HALF), 0)
    for q in range(9):
        tiles = []
        for c in range(2 * FREQ):
            table = cosine if c < FREQ else sine
            line = table[c % FREQ : c % FREQ + 1]
            front = jnp.broadcast_to(line[:, :HALF], (8, HALF))
            back = jnp.broadcast_to(line[:, HALF:], (8, HALF))
            tiles.append(jnp.where(slot == q, front, jnp.where(slot == q - 1, back, 0.0)))
        mark = 0 if q < 8 else 1
        tiles.append(jnp.where(slot == mark, 1.0, 0.0))
        tiles.append(jnp.zeros((8, HALF), F32))
        band_ref[:, q * HALF : (q + 1) * HALF] = jnp.concatenate(tiles, axis=0).astype(BF16)
    ones = jnp.ones((BAND, 128), BF16)
    sums_ref[...] = jnp.dot(band_ref[0:128, :], ones, preferred_element_type=F32)


def multiply_chunk(chunk, x_ref, band_ref, held_ref):
    band = band_ref[...]
    for g in range(GROUPS):
        x = x_ref[chunk, :, g * 8 * HALF : g * 8 * HALF + BAND]
        held_ref[chunk % 2, g] = lax.dot_general(band, x, NT, preferred_element_type=F32)


def finish_chunk(chunk, freqs, weights_ref, held_ref, sums_ref, parts_ref):
    held = held_ref.at[chunk % 2]
    total = held[GROUPS - 1, 129:130, :]
    for g in range(GROUPS):
        total = total + held[g, 128:129, :]
    mean = total * (1.0 / SAMPLES)
    w = jnp.concatenate([weights_ref[2 * chunk : 2 * chunk + 1], weights_ref[2 * chunk + 1 : 2 * chunk + 2]], axis=1)
    scale = jnp.sqrt(w * (1.0 / POINTS)) * (1.0 / math.sqrt(NB * 0.375 * NFFT))
    cols = slice(chunk * CHUNK, (chunk + 1) * CHUNK)
    for f in freqs:
        for part in range(2):
            rows = pl.ds(part * FREQ * 8 + f * 8 if isinstance(f, int) else pl.multiple_of(part * FREQ * 8 + f * 8, 8), 8)
            sums = sums_ref[rows, :]
            away = jnp.concatenate([sums, sums], axis=1) * mean
            y = jnp.concatenate([(held[g, rows, :] - away) * scale for g in range(GROUPS)], axis=0)
            hi = y.astype(BF16)
            lo = (y - hi.astype(F32)).astype(BF16)
            parts_ref[f, part * NB : (part + 1) * NB, cols] = hi
            parts_ref[f, 64 + part * NB : 64 + (part + 1) * NB, cols] = lo
            parts_ref[f, 128 + part * NB : 128 + (part + 1) * NB, cols] = hi


def add_gram(chunk, freqs, parts_ref, gram_ref):
    cols = slice(chunk * CHUNK, (chunk + 1) * CHUNK)
    for f in freqs:
        both = parts_ref[f, 0:128, cols]
        s = lax.dot_general(both, both, NT, preferred_element_type=F32)
        s = s[0:64] + s[64:128]
        gram_ref[f] = s if chunk == 0 else gram_ref[f] + s


def packed_gram(gram_ref, f):
    s = gram_ref[f]
    s = s[:, 0:64] + s[:, 64:128]
    gram_real = s[0:32, 0:32] + s[32:64, 32:64]
    gram_imag = s[0:32, 32:64] - s[32:64, 0:32]
    i = lax.broadcasted_iota(jnp.int32, (NB, NB), 0)
    j = lax.broadcasted_iota(jnp.int32, (NB, NB), 1)
    packed = jnp.where(i >= j, gram_real, gram_imag)
    return jnp.concatenate([packed[8 * r : 8 * r + 8] for r in range(4)], axis=1)


def lanes(tile, k):
    return jnp.broadcast_to(tile[:, k : k + 1], (8, 128))


def sublanes(tile, s):
    return jnp.broadcast_to(tile[s : s + 1], (8, 128))


def unpack_gram(packed):
    p = jnp.concatenate([packed[:, 32 * r : 32 * r + 32] for r in range(4)], axis=0)
    t = p.T
    i = lax.broadcasted_iota(jnp.int32, (NB, NB), 0)
    j = lax.broadcasted_iota(jnp.int32, (NB, NB), 1)
    real = jnp.where(i >= j, p, t)
    imag = jnp.where(i < j, p, jnp.where(i > j, -t, 0.0))
    eye = jnp.where(i == j, 1.0, 0.0)
    zero = jnp.zeros((NB, NB), F32)
    whole = jnp.concatenate([real, imag, eye, zero], axis=1)
    turned = jnp.concatenate([-imag, real, zero, eye], axis=1)
    return [whole[8 * u : 8 * u + 8] for u in range(4)], [turned[8 * u : 8 * u + 8] for u in range(4)]


def eliminate_panel(a, b, pivots, first):
    sub = lax.broadcasted_iota(jnp.int32, (8, 128), 0)
    v, s = first // 8, first % 8
    last = s + WIDTH == 8
    col_real = {u: [lanes(a[u], first + j) for j in range(WIDTH)] for u in range(v, 4)}
    col_imag = {u: [lanes(a[u], NB + first + j) for j in range(WIDTH)] for u in range(v, 4)}
    rows = [sublanes(a[v], s + j) for j in range(WIDTH)]
    turned = [sublanes(b[v], s + j) for j in range(WIDTH)]
    block_real = [[sublanes(col_real[v][l], s + i) for l in range(i + 1)] for i in range(WIDTH)]
    block_imag = [[sublanes(col_imag[v][l], s + i) for l in range(i)] for i in range(WIDTH)]
    over = []
    for j in range(WIDTH):
        pivot = block_real[j][j]
        inverse = 1.0 / pivot
        over.append(inverse)
        pivots[v] = jnp.where(sub == s + j, pivot, pivots[v])
        below = range(j + 1, WIDTH)
        m_real = {i: block_real[i][j] * inverse for i in below}
        m_imag = {i: block_imag[i][j] * inverse for i in below}
        for i in below:
            for l in range(j + 1, i + 1):
                other_real, other_imag = block_real[l][j], block_imag[l][j]
                block_real[i][l] = block_real[i][l] - (m_real[i] * other_real + m_imag[i] * other_imag)
                if l < i:
                    block_imag[i][l] = block_imag[i][l] - (m_imag[i] * other_real - m_real[i] * other_imag)
        for i in below:
            rows[i], turned[i] = (
                rows[i] - (m_real[i] * rows[j] + m_imag[i] * turned[j]),
                turned[i] - (m_real[i] * turned[j] - m_imag[i] * rows[j]),
            )
        for u in range(v + 1 if last else v, 4):
            x, y = col_real[u][j], col_imag[u][j]
            for l in below:
                col_real[u][l] = col_real[u][l] - (x * m_real[l] + y * m_imag[l])
                col_imag[u][l] = col_imag[u][l] - (y * m_real[l] - x * m_imag[l])
    for u in range(v, 4):
        new_a, new_b = a[u], b[u]
        if u > v or not last:
            for j in range(WIDTH):
                x, y = col_real[u][j], col_imag[u][j]
                row, row_turned = rows[j] * over[j], turned[j] * over[j]
                new_a = new_a - (x * row + y * row_turned)
                new_b = new_b - (x * row_turned - y * row)
            if u == v and s > 0:
                new_a = jnp.where(sub < s, a[u], new_a)
                new_b = jnp.where(sub < s, b[u], new_b)
        if u == v:
            for j in range(WIDTH):
                new_a = jnp.where(sub == s + j, rows[j], new_a)
                new_b = jnp.where(sub == s + j, turned[j], new_b)
        a[u], b[u] = new_a, new_b


def eliminate(packs):
    states = [unpack_gram(packed) for packed in packs]
    pivots = [[jnp.ones((8, 128), F32) for _ in range(4)] for _ in packs]
    for first in range(0, NB, WIDTH):
        for (a, b), pivot in zip(states, pivots):
            eliminate_panel(a, b, pivot, first)
    return [[a[u] * (1.0 / jnp.sqrt(pivot[u])) for u in range(4)] for (a, b), pivot in zip(states, pivots)]


def wait_bytes(ref, sem):
    pltpu.make_async_copy(ref, ref, sem).wait()


def gram_kernel(
    bins_ref, weights_ref, snap_ref, parts_ref, lower_ref, upper_ref,
    bins_here, weights_here, x_ref, band_ref, sums_ref, held_ref, gram_ref, pack_ref, got_s, got_x, got_p, all_upper,
    small_sem, in_sem, s_sems, x_sems, p_sems, c_sems, r_sems,
):
    x, share, core = place()
    sibling = (x, share * 2 + 1 - core)
    def send(src, dst, sems, device):
        pltpu.make_async_remote_copy(
            src_ref=src, dst_ref=dst, send_sem=sems.at[0], recv_sem=sems.at[1], device_id=device, device_id_type=MESH
        ).start()

    barrier = pltpu.get_barrier_semaphore()

    def greet(device):
        pl.semaphore_signal(barrier, inc=1, device_id=device, device_id_type=MESH)

    smalls = [
        pltpu.make_async_copy(bins_ref, bins_here, small_sem.at[0]),
        pltpu.make_async_copy(weights_ref, weights_here, small_sem.at[1]),
    ]
    for small in smalls:
        small.start()
    loads = [
        pltpu.make_async_copy(snap_ref.at[chunk * CHUNK : (chunk + 1) * CHUNK, :], x_ref.at[chunk], in_sem.at[chunk])
        for chunk in range(CHUNKS)
    ]
    loads[0].start()
    for step in PLANE_STEPS[:8]:
        greet(plane_peer(x, share, core, step)[1])
    loads[1].start()
    for step in PLANE_STEPS[8:]:
        greet(plane_peer(x, share, core, step)[1])
    for small in smalls:
        small.wait()
    build_band(bins_here, band_ref, sums_ref)
    for step in ROW_STEPS:
        greet(row_peer(x, share, core, step)[1])
    greet(sibling)
    loads[2].start()
    for chunk in range(CHUNKS):
        loads[chunk].wait()
        if chunk == 0:
            loads[3].start()
        multiply_chunk(chunk, x_ref, band_ref, held_ref)
        if chunk > 0:
            finish_chunk(chunk - 1, range(FREQ), weights_here, held_ref, sums_ref, parts_ref)
            add_gram(chunk - 1, range(FREQ), parts_ref, gram_ref)
    for side in range(2):
        freqs = [2 * n + (1 - core if side == 0 else core) for n in range(FREQ // 2)]
        finish_chunk(CHUNKS - 1, freqs, weights_here, held_ref, sums_ref, parts_ref)
        add_gram(CHUNKS - 1, freqs, parts_ref, gram_ref)
        for n in range(FREQ // 2):
            pack_ref[side, n] = packed_gram(gram_ref, freqs[n])
        if side == 0:
            pl.semaphore_wait(barrier, 1 + ROW - 1 + SHARES - 1)
            send(pack_ref.at[0], got_s, s_sems, sibling)
    wait_bytes(got_s, s_sems.at[1])
    got_x[x] = pack_ref[1] + got_s[...]

    for step in ROW_STEPS:
        send(got_x.at[x], got_x.at[x], x_sems, row_peer(x, share, core, step)[1])
    wait_bytes(got_x.at[0 : ROW - 1], x_sems.at[1])
    got_p[share] = (got_x[0] + got_x[1]) + (got_x[2] + got_x[3])

    for step in PLANE_STEPS:
        send(got_p.at[share], got_p.at[share], p_sems, plane_peer(x, share, core, step)[1])
    wait_bytes(got_p.at[0 : SHARES - 1], p_sems.at[1])
    packs = []
    for n in range(FREQ // 2):
        terms = [got_p[m, n] for m in range(SHARES)]
        while len(terms) > 1:
            terms = [terms[m] + terms[m + 1] for m in range(0, len(terms), 2)]
        packs.append(terms[0])

    lane = lax.broadcasted_iota(jnp.int32, (8, 128), 1)
    for n, rows in enumerate(eliminate(packs)):
        for h in range(2):
            even, odd = rows[2 * h], rows[2 * h + 1]
            odd_far = pltpu.roll(odd, 64, 1)
            lower_ref[core, n, h] = jnp.where(lane < 64, odd_far, even)
            all_upper[n, h] = jnp.where(lane < 64, even, odd_far)
    send(lower_ref.at[core], lower_ref.at[core], c_sems, sibling)
    upper_ref[core] = all_upper[x]
    send(upper_ref.at[core], upper_ref.at[core], r_sems, sibling)
    wait_bytes(lower_ref.at[0], c_sems.at[1])
    wait_bytes(upper_ref.at[0], r_sems.at[1])

    wait_bytes(got_s, s_sems.at[0])
    wait_bytes(got_x.at[0 : ROW - 1], x_sems.at[0])
    wait_bytes(got_p.at[0 : SHARES - 1], p_sems.at[0])
    wait_bytes(lower_ref.at[0], c_sems.at[0])
    wait_bytes(upper_ref.at[0], r_sems.at[0])


def modes_kernel(parts_ref, lower_ref, packed_ref, modes_ref, upper_ref, out_ref, up_ref, out_sem, up_sem):
    i = lax.broadcasted_iota(jnp.int32, (NB, NB), 0)
    j = lax.broadcasted_iota(jnp.int32, (NB, NB), 1)
    for n in range(2):
        both = jnp.concatenate(
            [packed_ref[n, 0][:, :64], packed_ref[n, 0][:, 64:], packed_ref[n, 1][:, :64], packed_ref[n, 1][:, 64:]], axis=0
        )
        up_ref[0, n] = jnp.where(j >= i, both[:, :32], 0.0)
        up_ref[1, n] = jnp.where(j > i, both[:, 32:], 0.0)
    up_store = pltpu.make_async_copy(up_ref, upper_ref, up_sem)
    up_store.start()
    stores = []
    for f in range(FREQ):
        low, high = lower_ref[f % 2, f // 2, 0], lower_ref[f % 2, f // 2, 1]
        inv = jnp.concatenate([low[:, 64:], low[:, :64], high[:, 64:], high[:, :64]], axis=0) * math.sqrt(POINTS)
        inv = jnp.concatenate([inv, jnp.concatenate([-inv[:, 32:], inv[:, :32]], axis=1)], axis=0)
        hi = inv.astype(BF16)
        lo = (inv - hi.astype(F32)).astype(BF16)
        left = jnp.concatenate([hi, hi, lo], axis=1)
        modes = jnp.dot(left, parts_ref[f], preferred_element_type=F32)
        out_ref[0, f] = modes[0:32]
        out_ref[1, f] = modes[32:64]
        store = pltpu.make_async_copy(out_ref.at[:, f], modes_ref.at[:, f], out_sem.at[f])
        store.start()
        stores.append(store)
    up_store.wait()
    for store in stores:
        store.wait()


def body(snapshots, weights, freq_bins):
    dma = pltpu.SemaphoreType.DMA
    hbm = pl.BlockSpec(memory_space=pltpu.HBM)
    vmem = pl.BlockSpec(memory_space=pltpu.VMEM)
    snapshots, weights, freq_bins = (pltpu.with_memory_space_constraint(a, pltpu.HBM) for a in (snapshots, weights.reshape(8, 128), freq_bins))
    parts, lower, upper = pl.pallas_call(
        gram_kernel,
        out_shape=(
            jax.ShapeDtypeStruct((FREQ, 192, LOCAL), BF16),
            jax.ShapeDtypeStruct((2, ROW, 2, 8, 128), F32),
            jax.ShapeDtypeStruct((2, 2, 8, 128), F32),
        ),
        in_specs=[hbm, hbm, hbm],
        out_specs=(vmem, vmem, vmem),
        scratch_shapes=[
            pltpu.SMEM((FREQ,), jnp.int32),
            pltpu.VMEM((8, 128), F32),
            pltpu.VMEM((CHUNKS, CHUNK, SAMPLES), BF16),
            pltpu.VMEM((ROWS, BAND), BF16),
            pltpu.VMEM((128, 128), F32),
            pltpu.VMEM((2, GROUPS, ROWS, CHUNK), F32),
            pltpu.VMEM((FREQ, 64, 128), F32),
            pltpu.VMEM((2, ROW, 8, 128), F32),
            pltpu.VMEM((ROW, 8, 128), F32),
            pltpu.VMEM((ROW, ROW, 8, 128), F32),
            pltpu.VMEM((SHARES, ROW, 8, 128), F32),
            pltpu.VMEM((ROW, 2, 8, 128), F32),
            dma((2,)), dma((CHUNKS,)),
            dma((2,)), dma((2,)), dma((2,)), dma((2,)), dma((2,)),
        ],
        compiler_params=pltpu.CompilerParams(
            collective_id=0, has_side_effects=True, vmem_limit_bytes=GRAM_MIB * 1024 * 1024
        ),
        cost_estimate=pl.CostEstimate(flops=2_000_000_000, bytes_accessed=11_000_000, transcendentals=0),
    )(freq_bins, weights, snapshots)
    return pl.pallas_call(
        modes_kernel,
        out_shape=(
            jax.ShapeDtypeStruct((2, FREQ, NB, LOCAL), F32),
            jax.ShapeDtypeStruct((2, 2, NB, NB), F32),
        ),
        in_specs=[vmem, vmem, vmem],
        out_specs=(hbm, hbm),
        scratch_shapes=[
            pltpu.VMEM((2, FREQ, NB, LOCAL), F32),
            pltpu.VMEM((2, 2, NB, NB), F32),
            dma((FREQ,)), dma,
        ],
        compiler_params=pltpu.CompilerParams(vmem_limit_bytes=MODES_MIB * 1024 * 1024),
        cost_estimate=pl.CostEstimate(flops=400_000_000, bytes_accessed=5_000_000, transcendentals=0),
    )(parts, lower, upper)


def solution(mesh):
    return jax.shard_map(
        body,
        mesh=mesh,
        in_specs=(P(("freq", "pts"), None), P(("freq", "pts")), P()),
        out_specs=(P(None, None, None, ("freq", "pts")), P(None, "freq", None, None)),
        check_vma=False,
    )
```
